256 devices in a mesh: tm: 4 (over x), pair: 64 (over z, y, core).
Axes of the slice: x: 4, y: 4, z: 8, core: 2. Of those that a mesh axis runs over, the one named last changes fastest.
Arguments:
- strain: bfloat16 [8, 8192, 8192], P('tm', 'pair'), may hold values from -80 to 80
- pair_list: int32 [4096, 2], replicated, may hold values from 0 to 4095, as said below
- pair_bins: int32 [4096], P('pair'), may hold values from 0 to 511, as said below
- bin_slots: int32 [512], replicated, may hold values from 0 to 511, as said below
- seg_valid: int32 [8], P('tm'), may hold values 0 or 1
Outputs:
- stacked: float32 [512, 2048], P('pair', 'tm')
The draws below stay inside these ranges and needn't reach their ends.
Inputs may be any that keep to these rules, and one draw needn't show every extreme that they name: `pair_list`: the 64 rows of one index of pair name, over both columns, exactly 2 different blocks of every device, block g lying on index g // 64; the two blocks of a pair differ. `pair_bins`: bin n belongs to index bin_slots[n] // 8 of pair. The rows of one index of pair name at most 3 pairs whose bins belong to one index; 8 indices receive exactly 3 from every index. `bin_slots`: A permutation of the stack's rows.
All inputs are finite; a program needn't handle non-finite values. No bound on the sum of `seg_valid` on one device may be relied on, other than what follows from the above.
Results may differ from the reference program's by a relative error of at most 0.011.
Values may be sent and summed in bfloat16 or wider, within the bound.
A program may use at most 128 MiB of HBM per device.

```python
import math
import jax
import jax.numpy as jnp
from jax import lax

SEG_LEN = 8192
BAND = 1024
FIRST_BIN = 128
WHITEN_BINS = 64
LAGS = 2048
BLOCK_CH = 2
CAPACITY = 3
BINS_DEV = 8
BLOCKS_DEV = 64
PAIRS_DEV = 64
SEGMENTS = 8
CHANNELS = 8192
BLOCKS = 4096
PAIRS = 4096
BINS = 512
HOT = 8
N_PAIR = 64


def draw_strain(key, part):
    key_base, key_gain = jax.random.split(key, 2)
    values = jax.random.uniform(key_base, (SEGMENTS, CHANNELS, SEG_LEN), jnp.float32, -1.7, 1.7)
    gains = jnp.exp(jax.random.uniform(key_gain, (1, CHANNELS, 1), jnp.float32, 0.0, math.log(10.0)))
    return (gains * values).astype(jnp.bfloat16)


def first_two(sub_key):
    return jax.random.permutation(sub_key, BLOCKS_DEV)[:2]


def one_device(dev_key):
    key_order, key_local = jax.random.split(dev_key)
    shuffled = jax.random.permutation(key_order, 2 * N_PAIR)
    sources = shuffled // 2
    copies = shuffled % 2
    picked = jax.vmap(first_two)(jax.random.split(key_local, N_PAIR))
    blocks = sources * BLOCKS_DEV + picked[sources, copies]
    return blocks.reshape(N_PAIR, 2)


def draw_pair_list(key, part):
    return jax.vmap(one_device)(jax.random.split(key, N_PAIR)).reshape(PAIRS, 2).astype(jnp.int32)


def bin_layout(key):
    key_all = jax.random.fold_in(key, 7)
    key_slot, key_owner, key_source = jax.random.split(key_all, 3)
    slots = jax.random.permutation(key_slot, BINS)
    owners = jax.random.permutation(key_owner, N_PAIR)
    hot_owners = owners[:HOT]
    cold_owners = owners[HOT:]

    def one_source(src_key):
        key_pick, key_mix, key_row = jax.random.split(src_key, 3)
        pool = jnp.tile(cold_owners, CAPACITY)
        chosen = jax.random.permutation(key_pick, pool)[:N_PAIR - CAPACITY * HOT]
        targets = jnp.concatenate([jnp.repeat(hot_owners, CAPACITY), chosen])
        targets = jax.random.permutation(key_mix, targets)
        rows_in = jax.random.randint(key_row, (N_PAIR,), 0, BINS_DEV)
        return targets * BINS_DEV + rows_in
    target_slots = jax.vmap(one_source)(jax.random.split(key_source, N_PAIR)).reshape(PAIRS)
    slot_to_bin = jnp.zeros((BINS,), jnp.int32).at[slots].set(jnp.arange(BINS, dtype=jnp.int32))
    return (slots.astype(jnp.int32), slot_to_bin[target_slots].astype(jnp.int32))


def draw_pair_bins(key, part):
    return bin_layout(key)[1]


def draw_bin_slots(key, part):
    return bin_layout(key)[0]


def touch_ends(result, stream_key, smallest, largest):
    shape = result.shape
    spot = [jax.random.randint(jax.random.fold_in(stream_key, axis), (), 0, shape[axis]) for axis in range(len(shape))]
    result = result.at[tuple(spot)].set(smallest)
    longest = shape.index(max(shape))
    spot[longest] = (spot[longest] + 1) % shape[longest]
    return result.at[tuple(spot)].set(largest)


def setup_inputs(seed: int = 0) -> dict:
    splits = jax.random.split(jax.random.key(seed), 6)
    strain = draw_strain(jax.random.fold_in(splits[5], 71), 0)
    pair_list = draw_pair_list(jax.random.fold_in(splits[5], 71), 0)
    pair_bins = draw_pair_bins(jax.random.fold_in(splits[5], 71), 0)
    bin_slots = draw_bin_slots(jax.random.fold_in(splits[5], 71), 0)
    seg_valid = touch_ends((jax.random.randint(splits[4], (SEGMENTS,), 0, 4) < 3).astype(jnp.int32), jax.random.fold_in(splits[4], 1), 0, 1)
    return {"strain": strain, "pair_list": pair_list, "pair_bins": pair_bins, "bin_slots": bin_slots, "seg_valid": seg_valid}


EPS = 1e-06

def forward_table(offset, length):
    sample_idx = offset + jnp.arange(length, dtype=jnp.int32)
    freq_idx = FIRST_BIN + jnp.arange(BAND, dtype=jnp.int32)
    phases = jnp.mod(sample_idx[:, None] * freq_idx[None, :], SEG_LEN).astype(jnp.float32) * (2.0 * math.pi / SEG_LEN)
    return jnp.concatenate([jnp.cos(phases), -jnp.sin(phases)], axis=1).astype(jnp.bfloat16)

def inverse_table(offset, length):
    lag_idx = offset + jnp.arange(length, dtype=jnp.int32) - LAGS // 2
    freq_idx = FIRST_BIN + jnp.arange(BAND, dtype=jnp.int32)
    phases = jnp.mod(freq_idx[:, None] * lag_idx[None, :], SEG_LEN).astype(jnp.float32) * (2.0 * math.pi / SEG_LEN)
    factor = 1.0 / math.sqrt(BAND)
    return jnp.concatenate([jnp.cos(phases) * factor, -jnp.sin(phases) * factor], axis=0)

def whiten(spectra):
    real_part = spectra[:, :BAND]
    imag_part = spectra[:, BAND:]
    powers = real_part * real_part + imag_part * imag_part
    energy = lax.optimization_barrier(jnp.mean(powers.reshape(powers.shape[0], BAND // WHITEN_BINS, WHITEN_BINS), axis=2))
    scaling = jnp.repeat(1.0 / jnp.sqrt(energy + EPS), WHITEN_BINS, axis=1)
    return jnp.concatenate([real_part * scaling, imag_part * scaling], axis=1).astype(jnp.bfloat16)

def cross_spectrum(left_side, right_side, weights):
    left_side = left_side.astype(jnp.float32)
    right_side = right_side.astype(jnp.float32)
    left_re = left_side[..., :BAND]
    left_im = left_side[..., BAND:]
    right_re = right_side[..., :BAND]
    right_im = right_side[..., BAND:]
    real_part = jnp.einsum('s,spcf->pf', weights, left_re * right_re + left_im * right_im, precision=lax.Precision.HIGHEST)
    imag_part = jnp.einsum('s,spcf->pf', weights, left_im * right_re - left_re * right_im, precision=lax.Precision.HIGHEST)
    return jnp.concatenate([real_part, imag_part], axis=1)

def reference(strain, pair_list, pair_bins, bin_slots, seg_valid):
    tables = forward_table(0, SEG_LEN)

    def transform(segment):
        return whiten(jnp.dot(segment, tables, preferred_element_type=jnp.float32))
    whitened = lax.map(transform, strain)
    whitened = whitened.reshape(SEGMENTS, BLOCKS, BLOCK_CH, 2 * BAND)
    weights = seg_valid.astype(jnp.float32)
    inverse = inverse_table(0, LAGS)
    targets = jnp.take(bin_slots, pair_bins).astype(jnp.int32)

    def one_group(running, group):
        pairs, rows_to = group
        left_side = jnp.take(whitened, pairs[:, 0], axis=1)
        right_side = jnp.take(whitened, pairs[:, 1], axis=1)
        cross_spec = cross_spectrum(left_side, right_side, weights)
        correlation = jnp.dot(cross_spec, inverse, precision=lax.Precision.HIGHEST, preferred_element_type=jnp.float32)
        return (running + jax.ops.segment_sum(correlation, rows_to, num_segments=BINS), None)
    stacked, _ = lax.scan(one_group, jnp.zeros((BINS, LAGS), jnp.float32), (pair_list.reshape(N_PAIR, PAIRS_DEV, 2), targets.reshape(N_PAIR, PAIRS_DEV)))
    return stacked
```

```python
import functools
import math

import jax
import jax.numpy as jnp
import numpy as np
from jax import lax
from jax.experimental import pallas as pl
from jax.experimental.pallas import tpu as pltpu
from jax.sharding import PartitionSpec as P

SEG_LEN = 8192
BAND = 1024
FIRST_BIN = 128
LAGS = 2048
EPS = 1e-06
NPAIR = 64
NTM = 4
SUB = SEG_LEN // 8
MESH = pl.DeviceIdType.MESH
F32 = jnp.float32
BF16 = jnp.bfloat16


def owned_bins():
    bins = np.zeros((4, 16, 2, 8), np.int64)
    for c in range(4):
        for a in range(2):
            k1 = (0, 4)[a] if c == 0 else (c, 8 - c)[a]
            for w in range(16):
                bins[c, w, a] = k1 + 8 * (16 + 8 * w + np.arange(8))
    return bins


def forward_tables():
    bins = owned_bins()
    t = np.arange(SUB, dtype=np.int64)
    theta = (bins[..., None] * t % SEG_LEN) * (2.0 * math.pi / SEG_LEN)
    cos, sin = np.cos(theta), np.sin(theta)
    table = np.zeros((4, 16, 2, 2, 8, 2, SUB), np.float64)
    sign = (1.0, -1.0)
    for c in range(4):
        for a in range(2):
            if c == 0:
                table[c, :, 0, a, :, a] = cos[c, :, a]
                table[c, :, 1, a, :, a] = -sin[c, :, a]
            else:
                table[c, :, 0, a, :, 0] = cos[c, :, a]
                table[c, :, 0, a, :, 1] = sign[a] * sin[c, :, a]
                table[c, :, 1, a, :, 0] = -sin[c, :, a]
                table[c, :, 1, a, :, 1] = sign[a] * cos[c, :, a]
    return table.reshape(4, 512, 2 * SUB).astype(jnp.bfloat16)


def inverse_tables():
    bins = owned_bins().reshape(NPAIR, 16)
    lag = np.arange(LAGS, dtype=np.int64) - LAGS // 2
    phi = (bins[..., None] * lag % SEG_LEN) * (2.0 * math.pi / SEG_LEN)
    factor = 1.0 / math.sqrt(BAND)
    table = np.stack([np.cos(phi) * factor, -np.sin(phi) * factor], axis=1)
    table = table.reshape(2 * BAND, NTM, LAGS // NTM).transpose(1, 0, 2)
    return np.ascontiguousarray(table).astype(jnp.bfloat16)


def fold_table():
    table = np.zeros((4, 2, 2, 2, 2, 16, 4, 2, 16), np.float32)
    for q in range(4):
        for b in range(16):
            table[q, 0, 0, :, :, b, q, 0, b] = 1.0
            table[q, 0, 1, :, :, b, q, 0, b] = 1.0
            table[q, 1, 0, :, :, b, q, 1, b] = -1.0
            table[q, 1, 1, :, :, b, q, 1, b] = 1.0
    return table.reshape(1024, 128).astype(jnp.bfloat16)


def iota(shape, dim):
    return lax.broadcasted_iota(jnp.int32, shape, dim)


def dot(a, b):
    return jnp.dot(a, b, preferred_element_type=F32)


def dot_nt(a, b):
    return lax.dot_general(a, b, (((1,), (1,)), ((), ())), preferred_element_type=F32)


def body(
    x_hbm, tab_hbm, inv_hbm, fold_ref, pairs_ref, bins_smem, slots_smem, valid_smem,
    out_ref,
    x_buf, tab_buf, inv_buf, y_buf, r_buf, send_buf, recv_buf, id_buf,
    src_rows, loc_rows, loc_mat, g1_buf, g2_buf, s_buf, rows_buf, p_buf,
    part_buf, got_buf, spec_buf,
    load_sem, send_sem, recv_sem, id_send, id_recv, part_send, part_recv, x_send, x_recv,
):
    tm = lax.axis_index("tm")
    me = lax.axis_index("pair")

    def x_load(s):
        return pltpu.make_async_copy(x_hbm.at[s], x_buf.at[s], load_sem.at[s])

    def tab_load(c):
        return pltpu.make_async_copy(tab_hbm.at[c], tab_buf.at[c], load_sem.at[2 + c])

    inv_load = pltpu.make_async_copy(inv_hbm.at[tm], inv_buf, load_sem.at[6])
    x_load(0).start()
    x_load(1).start()
    for c in range(4):
        tab_load(c).start()
    inv_load.start()

    barrier = pltpu.get_barrier_semaphore()

    def greet(i, _):
        pl.semaphore_signal(barrier, inc=1, device_id=(tm, lax.rem(me + i, NPAIR)), device_id_type=MESH)
        return 0

    lax.fori_loop(1, NPAIR, greet, 0)
    for i in range(1, NTM):
        pl.semaphore_signal(barrier, inc=1, device_id=(lax.rem(tm + i, NTM), me), device_id_type=MESH)

    lane = iota((1, 128), 1)
    first_lane = lax.rem(me, 2) * 64

    def one_id(k, row):
        r = slots_smem[bins_smem[k]]
        code = (r & 3) * 128 + (r >> 3) * 2 + ((r >> 2) & 1)
        return jnp.where(lane == first_lane + k, code, row)

    id_buf[me] = lax.fori_loop(0, 64, one_id, jnp.zeros((1, 128), jnp.int32))

    root = math.sqrt(0.5)
    for s in range(2):
        x_load(s).wait()

        def split(step, _):
            rows = pl.ds(pl.multiple_of(step * 16, 16), 16)
            to = pl.ds(pl.multiple_of(s * 128 + step * 16, 16), 16)
            for h in range(2):
                v = [
                    x_buf[s, rows, e * SUB + h * 512 : e * SUB + h * 512 + 512].astype(F32)
                    for e in range(8)
                ]
                s04, s26, s15, s37 = v[0] + v[4], v[2] + v[6], v[1] + v[5], v[3] + v[7]
                d04, d26, d15, d37 = v[0] - v[4], v[2] - v[6], v[1] - v[5], v[3] - v[7]
                even, odd = s04 + s26, s15 + s37
                diff, both = (d15 - d37) * root, (d15 + d37) * root
                parts = (
                    (even + odd, even - odd),
                    (d04 + diff, -d26 - both),
                    (s04 - s26, s37 - s15),
                    (d04 - diff, d26 - both),
                )
                for c in range(4):
                    for part in range(2):
                        at = part * SUB + h * 512
                        y_buf[c, to, at : at + 512] = parts[c][part].astype(BF16)
            return 0

        lax.fori_loop(0, 8, split, 0)

    for c in range(4):
        tab_load(c).wait()
        r_buf[c] = dot_nt(tab_buf[c], y_buf[c])

    def white(w, _):
        rows = pl.ds(pl.multiple_of(w * 32, 32), 32)
        parts = [r_buf[c, rows, :] for c in range(4)]
        power = parts[0] * parts[0]
        for c in range(1, 4):
            power = power + parts[c] * parts[c]
        energy = jnp.sum(power, axis=0, keepdims=True) * (1.0 / 64.0)
        scale = 1.0 / jnp.sqrt(energy + EPS)
        for c in range(4):
            done = (parts[c] * scale).astype(BF16)
            send_buf[c * 16 + w, 0:32, :] = done[:, 0:128]
            send_buf[c * 16 + w, 32:64, :] = done[:, 128:256]
        return 0

    lax.fori_loop(0, 16, white, 0)

    pl.semaphore_wait(barrier, NPAIR - 1 + NTM - 1)

    def id_copy(d):
        return pltpu.make_async_remote_copy(
            src_ref=id_buf.at[me], dst_ref=id_buf.at[me], send_sem=id_send.at[d],
            recv_sem=id_recv.at[me], device_id=(tm, d), device_id_type=MESH,
        )

    def main_copy(d):
        return pltpu.make_async_remote_copy(
            src_ref=send_buf.at[d], dst_ref=recv_buf.at[me], send_sem=send_sem.at[d],
            recv_sem=recv_sem.at[me], device_id=(tm, d), device_id_type=MESH,
        )

    def arrival(buf, sems, s):
        return pltpu.make_async_copy(buf.at[s], buf.at[s], sems.at[s])

    def send_all(i, _):
        d = lax.rem(me + i, NPAIR)
        id_copy(d).start()
        main_copy(d).start()
        return 0

    lax.fori_loop(1, NPAIR, send_all, 0)
    recv_buf[me] = send_buf[me]

    low = iota((1, 128), 1) < 64
    for q in range(32):
        a = pairs_ref[0:1, q * 128 : q * 128 + 128]
        b = pairs_ref[1:2, q * 128 : q * 128 + 128]
        first = jnp.where(low, a, pltpu.roll(b, 64, 1))
        second = jnp.where(low, pltpu.roll(a, 64, 1), b)
        for j, row in enumerate((first, second)):
            src_rows[2 * q + j : 2 * q + j + 1, :] = (row >> 6).astype(F32)
            loc_rows[2 * q + j : 2 * q + j + 1, :] = (row & 63).astype(F32)
    src_rows[64:128, :] = jnp.zeros((64, 128), F32)
    src_cols = src_rows[...].T.astype(BF16)
    lane_sq = iota((128, 128), 1)
    sub_sq = iota((128, 128), 0)
    lane_f = lane_sq.astype(F32)
    ones_sq = jnp.ones((128, 128), BF16)
    group = 8

    def ask(step, _):
        base = step * group
        pick = (iota((128, group * 128), 0) == base + iota((128, group * 128), 1) // 128)
        src_b = dot(src_cols, pick.astype(BF16))
        cols = [src_b[:, j * 128 : j * 128 + 128] for j in range(group)]
        earlier = []
        for j in range(group):
            row = src_rows[pl.ds(base + j, 1), :]
            hit = jnp.logical_and(cols[j] == row, lane_sq < sub_sq)
            earlier.append(jnp.where(hit, 1.0, 0.0).astype(BF16))
        slot_b = dot(jnp.concatenate(earlier, axis=0), ones_sq)
        for j in range(group):
            code = 2.0 * cols[j] + slot_b[j * 128 : j * 128 + 128]
            g2 = jnp.where(code == lane_f, 1.0, 0.0).astype(BF16)
            g2_buf[base + j] = g2
            loc = jnp.broadcast_to(loc_rows[pl.ds(base + j, 1), :], (16, 128)).astype(BF16)
            loc_mat[pl.ds(base + j, 1), :] = dot(loc, g2)[0:1, :]
        return 0

    lax.fori_loop(0, NPAIR // group, ask, 0)

    loc_cols = loc_mat[...].astype(BF16)

    def choose(s, _):
        pick = iota((128, 256), 0) == 2 * s + iota((128, 256), 1) // 128
        loc_b = dot(loc_cols, pick.astype(BF16))
        loc_b = 2.0 * jnp.concatenate([loc_b[:, 0:128], loc_b[:, 128:256]], axis=0)
        g1_buf[s, :, 0:128] = jnp.where(loc_b == lane_f, 1.0, 0.0).astype(BF16)
        g1_buf[s, :, 128:256] = jnp.where(loc_b + 1.0 == lane_f, 1.0, 0.0).astype(BF16)
        return 0

    lax.fori_loop(0, NPAIR, choose, 0, unroll=4)

    def id_wait(i, _):
        arrival(id_buf, id_recv, lax.rem(me + NPAIR - i, NPAIR)).wait()
        return 0

    lax.fori_loop(1, NPAIR, id_wait, 0)
    for q in range(32):
        row = id_buf[2 * q] + id_buf[2 * q + 1]
        hit = iota((512, 128), 0) == row
        s_buf[:, q * 128 : q * 128 + 128] = jnp.where(hit, 1.0, 0.0).astype(BF16)

    zero = jnp.zeros((16, 128), BF16)

    def take(i, _):
        s = lax.rem(me + NPAIR - i, NPAIR)

        @pl.when(i > 0)
        def _():
            arrival(recv_buf, recv_sem, s).wait()

        piece = [[recv_buf[s, (2 * g + ri) * 16 : (2 * g + ri) * 16 + 16, :] for ri in range(2)] for g in range(2)]
        rows = []
        for ri in range(2):
            for ch in range(2):
                for g in range(2):
                    halves = [piece[g][ri], zero] if ch == 0 else [zero, piece[g][ri]]
                    rows.append(jnp.concatenate(halves, axis=1))
        rows_buf[pl.ds(pl.multiple_of(s * 128, 128), 128), :] = dot_nt(
            g1_buf[s], jnp.concatenate(rows, axis=0)
        )
        return 0

    lax.fori_loop(0, NPAIR, take, 0)

    def cross(p, _):
        asked = rows_buf[pl.ds(p, 128, stride=64), :].astype(BF16)
        sides = dot(g2_buf[p], asked)
        left, right = sides[0:64], sides[64:128]
        to = pl.ds(pl.multiple_of(p * 64, 64), 64)
        p_buf[to, 0:128] = (left * right).astype(BF16)
        p_buf[to, 128:256] = (left * pltpu.roll(right, 64, 1)).astype(BF16)
        return 0

    lax.fori_loop(0, NPAIR, cross, 0, unroll=4)

    seg = (iota((1, 256), 1) >> 4) & 1
    weight = jnp.where(seg == 0, valid_smem[0], valid_smem[1]).astype(F32)
    total = jnp.zeros((128, 128), F32)
    for q in range(4):
        z = dot(s_buf[q * 128 : q * 128 + 128, :], p_buf[...]) * weight
        high = z.astype(BF16)
        rest = (z - high.astype(F32)).astype(BF16)
        fold = fold_ref[q * 256 : q * 256 + 256, :]
        total = total + (dot(high, fold) + dot(rest, fold))
    for d in range(NPAIR):
        part_buf[d] = total[2 * d : 2 * d + 2, :]

    def part_copy(d):
        return pltpu.make_async_remote_copy(
            src_ref=part_buf.at[d], dst_ref=got_buf.at[me], send_sem=part_send.at[d],
            recv_sem=part_recv.at[me], device_id=(tm, d), device_id_type=MESH,
        )

    def send_parts(i, _):
        part_copy(lax.rem(me + i, NPAIR)).start()
        return 0

    lax.fori_loop(1, NPAIR, send_parts, 0)
    got_buf[me] = part_buf[me]

    def part_wait(i, _):
        arrival(got_buf, part_recv, lax.rem(me + NPAIR - i, NPAIR)).wait()
        return 0

    lax.fori_loop(1, NPAIR, part_wait, 0)

    sub8, lane8 = iota((8, 128), 0), iota((8, 128), 1)
    for tile in range(16):
        made = jnp.zeros((8, 128), F32)
        for j in range(4):
            two = got_buf[4 * tile + j]
            both = jnp.where(
                sub8 < 4,
                jnp.broadcast_to(two[0:1, :], (8, 128)),
                jnp.broadcast_to(two[1:2, :], (8, 128)),
            )
            for q in range(4):
                turned = pltpu.roll(both, (32 * (j - q)) % 128, 1) if j != q else both
                here = jnp.logical_and(sub8 % 4 == q, lane8 // 32 == j)
                made = jnp.where(here, turned, made)
        spec_buf[tm, :, tile * 128 : tile * 128 + 128] = made

    def x_copy(i):
        to = lax.rem(tm + i, NTM)
        return pltpu.make_async_remote_copy(
            src_ref=spec_buf.at[tm], dst_ref=spec_buf.at[tm], send_sem=x_send.at[to],
            recv_sem=x_recv.at[tm], device_id=(to, me), device_id_type=MESH,
        )

    for i in range(1, NTM):
        x_copy(i).start()
    inv_load.wait()
    for i in range(1, NTM):
        arrival(spec_buf, x_recv, lax.rem(tm + NTM - i, NTM)).wait()
    spec = (spec_buf[0] + spec_buf[1]) + (spec_buf[2] + spec_buf[3])
    high = spec.astype(BF16)
    rest = (spec - high.astype(F32)).astype(BF16)
    lags = dot(jnp.concatenate([high, rest], axis=0), inv_buf[...])
    out_ref[...] = lags[0:8] + lags[8:16]

    def sent(i, _):
        d = lax.rem(me + i, NPAIR)
        id_copy(d).wait_send()
        main_copy(d).wait_send()
        part_copy(d).wait_send()
        return 0

    lax.fori_loop(1, NPAIR, sent, 0)
    for i in range(1, NTM):
        x_copy(i).wait_send()


def on_device(strain, pair_list, pair_bins, bin_slots, seg_valid):
    vmem = pl.BlockSpec(memory_space=pltpu.VMEM)
    smem = pl.BlockSpec(memory_space=pltpu.SMEM)
    hbm = pl.BlockSpec(memory_space=pl.ANY)
    dma = pltpu.SemaphoreType.DMA
    return pl.pallas_call(
        body,
        out_shape=jax.ShapeDtypeStruct((8, LAGS // NTM), F32),
        in_specs=[hbm, hbm, hbm, vmem, vmem, smem, smem, smem],
        out_specs=vmem,
        scratch_shapes=[
            pltpu.VMEM((2, 128, SEG_LEN), BF16),
            pltpu.VMEM((4, 512, 2 * SUB), BF16),
            pltpu.VMEM((2 * BAND, LAGS // NTM), BF16),
            pltpu.VMEM((4, 256, 2 * SUB), BF16),
            pltpu.VMEM((4, 512, 256), F32),
            pltpu.VMEM((NPAIR, 64, 128), BF16),
            pltpu.VMEM((NPAIR, 64, 128), BF16),
            pltpu.VMEM((NPAIR, 1, 128), jnp.int32),
            pltpu.VMEM((128, 128), F32),
            pltpu.VMEM((64, 128), F32),
            pltpu.VMEM((64, 128), F32),
            pltpu.VMEM((NPAIR, 128, 256), BF16),
            pltpu.VMEM((NPAIR, 128, 128), BF16),
            pltpu.VMEM((512, 4096), BF16),
            pltpu.VMEM((NPAIR * 128, 128), F32),
            pltpu.VMEM((4096, 256), BF16),
            pltpu.VMEM((NPAIR, 2, 128), F32),
            pltpu.VMEM((NPAIR, 2, 128), F32),
            pltpu.VMEM((NTM, 8, 2 * BAND), F32),
            dma((7,)), dma((NPAIR,)), dma((NPAIR,)), dma((NPAIR,)), dma((NPAIR,)),
            dma((NPAIR,)), dma((NPAIR,)), dma((NTM,)), dma((NTM,)),
        ],
        compiler_params=pltpu.CompilerParams(
            collective_id=0, has_side_effects=True, vmem_limit_bytes=60 << 20
        ),
    )(
        strain,
        jnp.asarray(forward_tables()),
        jnp.asarray(inverse_tables()),
        jnp.asarray(fold_table()),
        pair_list.T,
        pair_bins,
        bin_slots,
        seg_valid,
    )


def solution(mesh):
    return jax.shard_map(
        on_device,
        mesh=mesh,
        in_specs=(P("tm", "pair", None), P(), P("pair"), P(), P("tm")),
        out_specs=P("pair", "tm"),
        check_vma=False,
    )
```

```python
import functools
import math

import jax
import jax.numpy as jnp
import numpy as np
from jax import lax
from jax.experimental import pallas as pl
from jax.experimental.pallas import tpu as pltpu
from jax.sharding import PartitionSpec as P

SEG_LEN = 8192
BAND = 1024
FIRST_BIN = 128
LAGS = 2048
EPS = 1e-06
NPAIR = 64
NTM = 4
GROUP = 8
SUB = SEG_LEN // 8
MESH = pl.DeviceIdType.MESH
F32 = jnp.float32
BF16 = jnp.bfloat16


def owned_bins():
    bins = np.zeros((4, 16, 2, 8), np.int64)
    for c in range(4):
        for a in range(2):
            k1 = (0, 4)[a] if c == 0 else (c, 8 - c)[a]
            for w in range(16):
                bins[c, w, a] = k1 + 8 * (16 + 8 * w + np.arange(8))
    return bins


def forward_tables():
    bins = owned_bins()
    t = np.arange(SUB, dtype=np.int64)
    theta = (bins[..., None] * t % SEG_LEN) * (2.0 * math.pi / SEG_LEN)
    cos, sin = np.cos(theta), np.sin(theta)
    table = np.zeros((4, 16, 2, 2, 8, 2, SUB), np.float64)
    sign = (1.0, -1.0)
    for c in range(4):
        for a in range(2):
            if c == 0:
                table[c, :, 0, a, :, a] = cos[c, :, a]
                table[c, :, 1, a, :, a] = -sin[c, :, a]
            else:
                table[c, :, 0, a, :, 0] = cos[c, :, a]
                table[c, :, 0, a, :, 1] = sign[a] * sin[c, :, a]
                table[c, :, 1, a, :, 0] = -sin[c, :, a]
                table[c, :, 1, a, :, 1] = sign[a] * cos[c, :, a]
    return table.reshape(4, 512, 2 * SUB).astype(jnp.bfloat16)


def inverse_tables():
    bins = owned_bins().reshape(NPAIR, 16)
    lag = np.arange(LAGS, dtype=np.int64) - LAGS // 2
    phi = (bins[..., None] * lag % SEG_LEN) * (2.0 * math.pi / SEG_LEN)
    factor = 1.0 / math.sqrt(BAND)
    table = np.stack([np.cos(phi) * factor, -np.sin(phi) * factor], axis=1)
    table = table.reshape(2 * BAND, NTM, LAGS // NTM).transpose(1, 0, 2)
    return np.ascontiguousarray(table).astype(jnp.bfloat16)


def fold_table():
    table = np.zeros((4, 2, 2, 2, 2, 16, 4, 2, 16), np.float32)
    for q in range(4):
        for b in range(16):
            table[q, 0, 0, :, :, b, q, 0, b] = 1.0
            table[q, 0, 1, :, :, b, q, 0, b] = 1.0
            table[q, 1, 0, :, :, b, q, 1, b] = -1.0
            table[q, 1, 1, :, :, b, q, 1, b] = 1.0
    return table.reshape(1024, 128).astype(jnp.bfloat16)


def iota(shape, dim):
    return lax.broadcasted_iota(jnp.int32, shape, dim)


def dot(a, b):
    return jnp.dot(a, b, preferred_element_type=F32)


def dot_nt(a, b):
    return lax.dot_general(a, b, (((1,), (1,)), ((), ())), preferred_element_type=F32)


def body(
    x_hbm, tab_hbm, inv_hbm, fold_ref, pairs_ref, bins_smem, slots_smem, valid_smem,
    out_ref,
    x_buf, tab_buf, inv_buf, y_buf, r_buf, send_buf, recv_buf, id_buf,
    src_rows, loc_rows, loc_mat, g1_buf, g2_buf, s_buf, rows_buf, p_buf,
    part_buf, mid_buf, got_buf, spec_buf,
    load_sem, send_sem, recv_sem, id_sem, part_sem, x_sem,
):
    tm = lax.axis_index("tm")
    me = lax.axis_index("pair")

    def x_load(s):
        return pltpu.make_async_copy(x_hbm.at[s], x_buf.at[s], load_sem.at[s])

    def tab_load(c):
        return pltpu.make_async_copy(tab_hbm.at[c], tab_buf.at[c], load_sem.at[2 + c])

    inv_load = pltpu.make_async_copy(inv_hbm.at[tm], inv_buf, load_sem.at[6])
    x_load(0).start()
    x_load(1).start()
    for c in range(4):
        tab_load(c).start()
    inv_load.start()

    barrier = pltpu.get_barrier_semaphore()

    def greet(i, _):
        pl.semaphore_signal(barrier, inc=1, device_id=(tm, lax.rem(me + i, NPAIR)), device_id_type=MESH)
        return 0

    lax.fori_loop(1, NPAIR, greet, 0)
    for i in range(1, NTM):
        pl.semaphore_signal(barrier, inc=1, device_id=(lax.rem(tm + i, NTM), me), device_id_type=MESH)

    lane = iota((1, 128), 1)
    first_lane = lax.rem(me, 2) * 64

    def one_id(k, row):
        r = slots_smem[bins_smem[k]]
        code = (r & 3) * 128 + (r >> 3) * 2 + ((r >> 2) & 1)
        return jnp.where(lane == first_lane + k, code, row)

    id_buf[me] = lax.fori_loop(0, 64, one_id, jnp.zeros((1, 128), jnp.int32))

    root = math.sqrt(0.5)
    for s in range(2):
        x_load(s).wait()

        def split(step, _):
            rows = pl.ds(pl.multiple_of(step * 16, 16), 16)
            to = pl.ds(pl.multiple_of(s * 128 + step * 16, 16), 16)
            for h in range(2):
                v = [
                    x_buf[s, rows, e * SUB + h * 512 : e * SUB + h * 512 + 512].astype(F32)
                    for e in range(8)
                ]
                s04, s26, s15, s37 = v[0] + v[4], v[2] + v[6], v[1] + v[5], v[3] + v[7]
                d04, d26, d15, d37 = v[0] - v[4], v[2] - v[6], v[1] - v[5], v[3] - v[7]
                even, odd = s04 + s26, s15 + s37
                diff, both = (d15 - d37) * root, (d15 + d37) * root
                parts = (
                    (even + odd, even - odd),
                    (d04 + diff, -d26 - both),
                    (s04 - s26, s37 - s15),
                    (d04 - diff, d26 - both),
                )
                for c in range(4):
                    for part in range(2):
                        at = part * SUB + h * 512
                        y_buf[c, to, at : at + 512] = parts[c][part].astype(BF16)
            return 0

        lax.fori_loop(0, 8, split, 0)

    for c in range(4):
        tab_load(c).wait()
        r_buf[c] = dot_nt(tab_buf[c], y_buf[c])

    def white(w, _):
        rows = pl.ds(pl.multiple_of(w * 32, 32), 32)
        parts = [r_buf[c, rows, :] for c in range(4)]
        power = parts[0] * parts[0]
        for c in range(1, 4):
            power = power + parts[c] * parts[c]
        energy = jnp.sum(power, axis=0, keepdims=True) * (1.0 / 64.0)
        scale = 1.0 / jnp.sqrt(energy + EPS)
        for c in range(4):
            done = (parts[c] * scale).astype(BF16)
            send_buf[c * 16 + w, 0:32, :] = done[:, 0:128]
            send_buf[c * 16 + w, 32:64, :] = done[:, 128:256]
        return 0

    lax.fori_loop(0, 16, white, 0)

    pl.semaphore_wait(barrier, NPAIR - 1 + NTM - 1)

    here = me // GROUP * GROUP
    mine = lax.rem(me, GROUP)

    def beside(i):
        return here + lax.rem(mine + i, GROUP)

    def across(i):
        return lax.rem(me + i * GROUP, NPAIR)

    def remote(src, dst, sems, to):
        return pltpu.make_async_remote_copy(
            src_ref=src, dst_ref=dst, send_sem=sems[0], recv_sem=sems[1],
            device_id=to, device_id_type=MESH,
        )

    def landed(ref, sem):
        return pltpu.make_async_copy(ref, ref, sem)

    def main_copy(i):
        d = lax.rem(me + i, NPAIR)
        return remote(send_buf.at[d], recv_buf.at[me], (send_sem, recv_sem.at[me]), (tm, d))

    def send_main(i, _):
        main_copy(i).start()
        return 0

    for i in range(1, GROUP):
        remote(id_buf.at[me], id_buf.at[me], (id_sem.at[0], id_sem.at[1]), (tm, beside(i))).start()
    lax.fori_loop(1, 32, send_main, 0)
    landed(id_buf.at[pl.ds(0, GROUP - 1)], id_sem.at[1]).wait()
    own_group = id_buf.at[pl.ds(here, GROUP)]
    for i in range(1, GROUP):
        remote(own_group, own_group, (id_sem.at[2], id_sem.at[3]), (tm, across(i))).start()
    lax.fori_loop(32, NPAIR, send_main, 0)
    recv_buf[me] = send_buf[me]

    low = iota((1, 128), 1) < 64
    for q in range(32):
        a = pairs_ref[0:1, q * 128 : q * 128 + 128]
        b = pairs_ref[1:2, q * 128 : q * 128 + 128]
        first = jnp.where(low, a, pltpu.roll(b, 64, 1))
        second = jnp.where(low, pltpu.roll(a, 64, 1), b)
        for j, row in enumerate((first, second)):
            src_rows[2 * q + j : 2 * q + j + 1, :] = (row >> 6).astype(F32)
            loc_rows[2 * q + j : 2 * q + j + 1, :] = (row & 63).astype(F32)
    src_rows[64:128, :] = jnp.zeros((64, 128), F32)
    src_cols = src_rows[...].T.astype(BF16)
    lane_sq = iota((128, 128), 1)
    sub_sq = iota((128, 128), 0)
    lane_f = lane_sq.astype(F32)
    ones_sq = jnp.ones((128, 128), BF16)
    asks = 8

    def ask(step, _):
        base = step * asks
        pick = (iota((128, asks * 128), 0) == base + iota((128, asks * 128), 1) // 128)
        src_b = dot(src_cols, pick.astype(BF16))
        cols = [src_b[:, j * 128 : j * 128 + 128] for j in range(asks)]
        earlier = []
        for j in range(asks):
            row = src_rows[pl.ds(base + j, 1), :]
            hit = jnp.logical_and(cols[j] == row, lane_sq < sub_sq)
            earlier.append(jnp.where(hit, 1.0, 0.0).astype(BF16))
        slot_b = dot(jnp.concatenate(earlier, axis=0), ones_sq)
        for j in range(asks):
            code = 2.0 * cols[j] + slot_b[j * 128 : j * 128 + 128]
            g2 = jnp.where(code == lane_f, 1.0, 0.0).astype(BF16)
            g2_buf[base + j] = g2
            loc = jnp.broadcast_to(loc_rows[pl.ds(base + j, 1), :], (16, 128)).astype(BF16)
            loc_mat[pl.ds(base + j, 1), :] = dot(loc, g2)[0:1, :]
        return 0

    lax.fori_loop(0, NPAIR // asks, ask, 0)

    loc_cols = loc_mat[...].astype(BF16)

    def choose(s, _):
        pick = iota((128, 256), 0) == 2 * s + iota((128, 256), 1) // 128
        loc_b = dot(loc_cols, pick.astype(BF16))
        loc_b = 2.0 * jnp.concatenate([loc_b[:, 0:128], loc_b[:, 128:256]], axis=0)
        g1_buf[s, :, 0:128] = jnp.where(loc_b == lane_f, 1.0, 0.0).astype(BF16)
        g1_buf[s, :, 128:256] = jnp.where(loc_b + 1.0 == lane_f, 1.0, 0.0).astype(BF16)
        return 0

    lax.fori_loop(0, NPAIR, choose, 0, unroll=4)

    landed(id_buf.at[pl.ds(0, NPAIR - GROUP)], id_sem.at[3]).wait()
    for q in range(32):
        row = id_buf[2 * q] + id_buf[2 * q + 1]
        hit = iota((512, 128), 0) == row
        s_buf[:, q * 128 : q * 128 + 128] = jnp.where(hit, 1.0, 0.0).astype(BF16)

    zero = jnp.zeros((16, 128), BF16)

    batch = 4

    def take(step, _):
        first = step * batch
        sources = [lax.rem(me + NPAIR - first - j, NPAIR) for j in range(batch)]
        for j, s in enumerate(sources):
            if j == 0:

                @pl.when(first > 0)
                def _():
                    landed(recv_buf.at[s], recv_sem.at[s]).wait()

            else:
                landed(recv_buf.at[s], recv_sem.at[s]).wait()
        for s in sources:
            rows = []
            for ri in range(2):
                for ch in range(2):
                    for g in range(2):
                        at = (2 * g + ri) * 16
                        piece = recv_buf[s, at : at + 16, :]
                        halves = [piece, zero] if ch == 0 else [zero, piece]
                        rows.append(jnp.concatenate(halves, axis=1))
            rows_buf[pl.ds(pl.multiple_of(s * 128, 128), 128), :] = dot_nt(
                g1_buf[s], jnp.concatenate(rows, axis=0)
            )
        return 0

    lax.fori_loop(0, NPAIR // batch, take, 0)

    def cross(p, _):
        asked = rows_buf[pl.ds(p, 128, stride=64), :].astype(BF16)
        sides = dot(g2_buf[p], asked)
        left, right = sides[0:64], sides[64:128]
        to = pl.ds(pl.multiple_of(p * 64, 64), 64)
        p_buf[to, 0:128] = (left * right).astype(BF16)
        p_buf[to, 128:256] = (left * pltpu.roll(right, 64, 1)).astype(BF16)
        return 0

    lax.fori_loop(0, NPAIR, cross, 0, unroll=8)

    seg = (iota((1, 256), 1) >> 4) & 1
    weight = jnp.where(seg == 0, valid_smem[0], valid_smem[1]).astype(F32)
    total = jnp.zeros((128, 128), F32)
    for q in range(4):
        z = dot(s_buf[q * 128 : q * 128 + 128, :], p_buf[...]) * weight
        high = z.astype(BF16)
        rest = (z - high.astype(F32)).astype(BF16)
        fold = fold_ref[q * 256 : q * 256 + 256, :]
        total = total + (dot(high, fold) + dot(rest, fold))
    for d in range(NPAIR):
        part_buf[d // GROUP, d % GROUP] = total[2 * d : 2 * d + 2, :]

    group = me // GROUP
    for i in range(1, GROUP):
        to = across(i)
        remote(part_buf.at[to // GROUP], mid_buf.at[group], (part_sem.at[0], part_sem.at[1]), (tm, to)).start()
    mid_buf[group] = part_buf[group]
    landed(mid_buf.at[pl.ds(0, GROUP - 1)], part_sem.at[1]).wait()
    for i in range(1, GROUP):
        to = beside(i)
        remote(mid_buf.at[:, lax.rem(to, GROUP)], got_buf.at[:, mine], (part_sem.at[2], part_sem.at[3]), (tm, to)).start()
    got_buf[:, pl.ds(mine, 1)] = mid_buf[:, pl.ds(mine, 1)]
    landed(got_buf.at[:, pl.ds(0, GROUP - 1)], part_sem.at[3]).wait()

    sub8, lane8 = iota((8, 128), 0), iota((8, 128), 1)
    def spread(tile):
        made = jnp.zeros((8, 128), F32)
        for j in range(4):
            d = 4 * tile + j
            two = got_buf[d // GROUP, d % GROUP]
            both = jnp.where(
                sub8 < 4,
                jnp.broadcast_to(two[0:1, :], (8, 128)),
                jnp.broadcast_to(two[1:2, :], (8, 128)),
            )
            for q in range(4):
                turned = pltpu.roll(both, (32 * (j - q)) % 128, 1) if j != q else both
                fits = jnp.logical_and(sub8 % 4 == q, lane8 // 32 == j)
                made = jnp.where(fits, turned, made)
        return made

    for tile in range(8):
        both = jnp.concatenate([spread(tile), spread(tile + 8)], axis=0)
        spec_buf[tm, :, tile * 128 : tile * 128 + 128] = both.astype(BF16)

    own_spec = spec_buf.at[tm]
    for i in range(1, NTM):
        remote(own_spec, own_spec, (x_sem.at[0], x_sem.at[1]), (lax.rem(tm + i, NTM), me)).start()
    inv_load.wait()
    landed(spec_buf.at[pl.ds(0, NTM - 1)], x_sem.at[1]).wait()
    planes = [spec_buf[i].astype(F32) for i in range(NTM)]
    spec = (planes[0] + planes[1]) + (planes[2] + planes[3])
    high = spec.astype(BF16)
    rest = (spec - high.astype(F32)).astype(BF16)
    lags = dot(jnp.concatenate([high[0:8], rest[0:8]], axis=0), inv_buf[0:1024, :])
    lags = lags + dot(jnp.concatenate([high[8:16], rest[8:16]], axis=0), inv_buf[1024:2048, :])
    out_ref[...] = lags

    landed(send_buf.at[pl.ds(0, NPAIR - 1)], send_sem).wait()
    landed(id_buf.at[pl.ds(0, GROUP - 1)], id_sem.at[0]).wait()
    landed(id_buf.at[pl.ds(0, NPAIR - GROUP)], id_sem.at[2]).wait()
    landed(mid_buf.at[pl.ds(0, GROUP - 1)], part_sem.at[0]).wait()
    landed(got_buf.at[:, pl.ds(0, GROUP - 1)], part_sem.at[2]).wait()
    landed(spec_buf.at[pl.ds(0, NTM - 1)], x_sem.at[0]).wait()


def on_device(strain, pair_list, pair_bins, bin_slots, seg_valid):
    vmem = pl.BlockSpec(memory_space=pltpu.VMEM)
    smem = pl.BlockSpec(memory_space=pltpu.SMEM)
    hbm = pl.BlockSpec(memory_space=pl.ANY)
    dma = pltpu.SemaphoreType.DMA
    both = pl.pallas_call(
        body,
        out_shape=jax.ShapeDtypeStruct((16, LAGS // NTM), F32),
        in_specs=[hbm, hbm, hbm, vmem, vmem, smem, smem, smem],
        out_specs=vmem,
        scratch_shapes=[
            pltpu.VMEM((2, 128, SEG_LEN), BF16),
            pltpu.VMEM((4, 512, 2 * SUB), BF16),
            pltpu.VMEM((2 * BAND, LAGS // NTM), BF16),
            pltpu.VMEM((4, 256, 2 * SUB), BF16),
            pltpu.VMEM((4, 512, 256), F32),
            pltpu.VMEM((NPAIR, 64, 128), BF16),
            pltpu.VMEM((NPAIR, 64, 128), BF16),
            pltpu.VMEM((NPAIR, 1, 128), jnp.int32),
            pltpu.VMEM((128, 128), F32),
            pltpu.VMEM((64, 128), F32),
            pltpu.VMEM((64, 128), F32),
            pltpu.VMEM((NPAIR, 128, 256), BF16),
            pltpu.VMEM((NPAIR, 128, 128), BF16),
            pltpu.VMEM((512, 4096), BF16),
            pltpu.VMEM((NPAIR * 128, 128), F32),
            pltpu.VMEM((4096, 256), BF16),
            pltpu.VMEM((GROUP, GROUP, 2, 128), F32),
            pltpu.VMEM((GROUP, GROUP, 2, 128), F32),
            pltpu.VMEM((GROUP, GROUP, 2, 128), F32),
            pltpu.VMEM((NTM, 16, BAND), BF16),
            dma((7,)), dma, dma((NPAIR,)), dma((4,)), dma((4,)), dma((2,)),
        ],
        compiler_params=pltpu.CompilerParams(
            collective_id=0, has_side_effects=True, vmem_limit_bytes=60 << 20
        ),
    )(
        strain,
        jnp.asarray(forward_tables()),
        jnp.asarray(inverse_tables()),
        jnp.asarray(fold_table()),
        pair_list.T,
        pair_bins,
        bin_slots,
        seg_valid,
    )
    return both[0:8] + both[8:16]


def solution(mesh):
    return jax.shard_map(
        on_device,
        mesh=mesh,
        in_specs=(P("tm", "pair", None), P(), P("pair"), P(), P("tm")),
        out_specs=P("pair", "tm"),
        check_vma=False,
    )
```

```python
import functools
import math

import jax
import jax.numpy as jnp
import numpy as np
from jax import lax
from jax.experimental import pallas as pl
from jax.experimental.pallas import tpu as pltpu
from jax.sharding import PartitionSpec as P

SEG_LEN = 8192
BAND = 1024
FIRST_BIN = 128
LAGS = 2048
EPS = 1e-06
NPAIR = 64
NTM = 4
STEP = 129
GROUP = 8
SUB = SEG_LEN // 8
MESH = pl.DeviceIdType.MESH
F32 = jnp.float32
BF16 = jnp.bfloat16


def owned_bins():
    bins = np.zeros((4, 16, 2, 8), np.int64)
    for c in range(4):
        for a in range(2):
            k1 = (0, 4)[a] if c == 0 else (c, 8 - c)[a]
            for w in range(16):
                bins[c, w, a] = k1 + 8 * (16 + 8 * w + np.arange(8))
    return bins


def forward_tables():
    bins = owned_bins()
    t = np.arange(SUB, dtype=np.int64)
    theta = (bins[..., None] * t % SEG_LEN) * (2.0 * math.pi / SEG_LEN)
    cos, sin = np.cos(theta), np.sin(theta)
    table = np.zeros((4, 16, 2, 2, 8, 2, SUB), np.float64)
    sign = (1.0, -1.0)
    for c in range(4):
        for a in range(2):
            if c == 0:
                table[c, :, 0, a, :, a] = cos[c, :, a]
                table[c, :, 1, a, :, a] = -sin[c, :, a]
            else:
                table[c, :, 0, a, :, 0] = cos[c, :, a]
                table[c, :, 0, a, :, 1] = sign[a] * sin[c, :, a]
                table[c, :, 1, a, :, 0] = -sin[c, :, a]
                table[c, :, 1, a, :, 1] = sign[a] * cos[c, :, a]
    return table.reshape(4, 512, 2 * SUB).astype(jnp.bfloat16)


def inverse_tables():
    bins = owned_bins().reshape(NPAIR, 16)
    lag = np.arange(LAGS, dtype=np.int64) - LAGS // 2
    phi = (bins[..., None] * lag % SEG_LEN) * (2.0 * math.pi / SEG_LEN)
    factor = 1.0 / math.sqrt(BAND)
    table = np.stack([np.cos(phi) * factor, -np.sin(phi) * factor], axis=1)
    table = table.reshape(2 * BAND, NTM, LAGS // NTM).transpose(1, 0, 2)
    return np.ascontiguousarray(table).astype(jnp.bfloat16)


def fold_table():
    table = np.zeros((4, 2, 2, 2, 2, 16, 4, 2, 16), np.float32)
    for q in range(4):
        for b in range(16):
            table[q, 0, 0, :, :, b, q, 0, b] = 1.0
            table[q, 0, 1, :, :, b, q, 0, b] = 1.0
            table[q, 1, 0, :, :, b, q, 1, b] = -1.0
            table[q, 1, 1, :, :, b, q, 1, b] = 1.0
    return table.reshape(1024, 128).astype(jnp.bfloat16)


def iota(shape, dim):
    return lax.broadcasted_iota(jnp.int32, shape, dim)


def dot(a, b):
    return jnp.dot(a, b, preferred_element_type=F32)


def dot_nt(a, b):
    return lax.dot_general(a, b, (((1,), (1,)), ((), ())), preferred_element_type=F32)


def body(
    x_hbm, tab_hbm, inv_hbm, fold_ref, pairs_ref, bins_smem, slots_smem, valid_smem,
    out_ref,
    x_buf, tab_buf, inv_buf, y_buf, r_buf, send_buf, recv_buf, id_buf,
    src_rows, loc_rows, loc_mat, g1_buf, g2_buf, s_buf, rows_buf, p_buf,
    part_buf, got_buf, spec_buf,
    load_sem, send_sem, recv_sem, id_sem, part_sem, x_sem,
):
    tm = lax.axis_index("tm")
    me = lax.axis_index("pair")

    def x_load(s):
        return pltpu.make_async_copy(x_hbm.at[s], x_buf.at[s], load_sem.at[s])

    def tab_load(c):
        return pltpu.make_async_copy(tab_hbm.at[c], tab_buf.at[c], load_sem.at[2 + c])

    inv_load = pltpu.make_async_copy(inv_hbm.at[tm], inv_buf, load_sem.at[6])
    x_load(0).start()
    x_load(1).start()
    for c in range(4):
        tab_load(c).start()
    inv_load.start()

    barrier = pltpu.get_barrier_semaphore()

    def greet(i, _):
        pl.semaphore_signal(barrier, inc=1, device_id=(tm, lax.rem(me + i, NPAIR)), device_id_type=MESH)
        return 0

    lax.fori_loop(1, NPAIR, greet, 0)
    for i in range(1, NTM):
        pl.semaphore_signal(barrier, inc=1, device_id=(lax.rem(tm + i, NTM), me), device_id_type=MESH)

    lane = iota((1, 128), 1)
    first_lane = lax.rem(me, 2) * 64

    def one_id(k, row):
        r = slots_smem[bins_smem[k]]
        code = (r & 3) * 128 + (r >> 3) * 2 + ((r >> 2) & 1)
        return jnp.where(lane == first_lane + k, code, row)

    id_buf[me] = lax.fori_loop(0, 64, one_id, jnp.zeros((1, 128), jnp.int32))

    root = math.sqrt(0.5)
    for s in range(2):
        x_load(s).wait()

        def split(step, _):
            rows = pl.ds(pl.multiple_of(step * 16, 16), 16)
            to = pl.ds(pl.multiple_of(s * 128 + step * 16, 16), 16)
            for h in range(2):
                v = [
                    x_buf[s, rows, e * SUB + h * 512 : e * SUB + h * 512 + 512].astype(F32)
                    for e in range(8)
                ]
                s04, s26, s15, s37 = v[0] + v[4], v[2] + v[6], v[1] + v[5], v[3] + v[7]
                d04, d26, d15, d37 = v[0] - v[4], v[2] - v[6], v[1] - v[5], v[3] - v[7]
                even, odd = s04 + s26, s15 + s37
                diff, both = (d15 - d37) * root, (d15 + d37) * root
                parts = (
                    (even + odd, even - odd),
                    (d04 + diff, -d26 - both),
                    (s04 - s26, s37 - s15),
                    (d04 - diff, d26 - both),
                )
                for c in range(4):
                    for part in range(2):
                        at = part * SUB + h * 512
                        y_buf[c, to, at : at + 512] = parts[c][part].astype(BF16)
            return 0

        lax.fori_loop(0, 8, split, 0)

    for c in range(4):
        tab_load(c).wait()
        r_buf[c] = dot_nt(tab_buf[c], y_buf[c])

    def white(w, _):
        rows = pl.ds(pl.multiple_of(w * 32, 32), 32)
        parts = [r_buf[c, rows, :] for c in range(4)]
        power = parts[0] * parts[0]
        for c in range(1, 4):
            power = power + parts[c] * parts[c]
        energy = jnp.sum(power, axis=0, keepdims=True) * (1.0 / 64.0)
        scale = 1.0 / jnp.sqrt(energy + EPS)
        for c in range(4):
            done = (parts[c] * scale).astype(BF16)
            send_buf[c * 16 + w, 0:32, :] = done[:, 0:128]
            send_buf[c * 16 + w, 32:64, :] = done[:, 128:256]
        return 0

    lax.fori_loop(0, 16, white, 0)

    pl.semaphore_wait(barrier, NPAIR - 1 + NTM - 1)

    here = me // GROUP * GROUP
    mine = lax.rem(me, GROUP)

    def beside(i):
        return here + lax.rem(mine + i, GROUP)

    def across(i):
        return lax.rem(me + i * GROUP, NPAIR)

    def remote(src, dst, sems, to):
        return pltpu.make_async_remote_copy(
            src_ref=src, dst_ref=dst, send_sem=sems[0], recv_sem=sems[1],
            device_id=to, device_id_type=MESH,
        )

    def landed(ref, sem):
        return pltpu.make_async_copy(ref, ref, sem)

    def offset(n):
        return (32 + n // 2 * (1 - n % 2 * 2)) * jnp.minimum(n, 1)

    def main_copy(n):
        d = lax.rem(me + offset(n), NPAIR)
        return remote(send_buf.at[d], recv_buf.at[me], (send_sem, recv_sem.at[me]), (tm, d))

    def send_main(i, _):
        main_copy(i).start()
        return 0

    for i in range(1, GROUP):
        remote(id_buf.at[me], id_buf.at[me], (id_sem.at[0], id_sem.at[1]), (tm, beside(i))).start()
    lax.fori_loop(1, 32, send_main, 0)
    landed(id_buf.at[pl.ds(0, GROUP - 1)], id_sem.at[1]).wait()
    own_group = id_buf.at[pl.ds(here, GROUP)]
    for i in range(1, GROUP):
        remote(own_group, own_group, (id_sem.at[2], id_sem.at[3]), (tm, across(i))).start()
    lax.fori_loop(32, NPAIR, send_main, 0)
    recv_buf[me] = send_buf[me]

    low = iota((1, 128), 1) < 64
    for q in range(32):
        a = pairs_ref[0:1, q * 128 : q * 128 + 128]
        b = pairs_ref[1:2, q * 128 : q * 128 + 128]
        first = jnp.where(low, a, pltpu.roll(b, 64, 1))
        second = jnp.where(low, pltpu.roll(a, 64, 1), b)
        for j, row in enumerate((first, second)):
            src_rows[2 * q + j : 2 * q + j + 1, :] = (row >> 6).astype(F32)
            loc_rows[2 * q + j : 2 * q + j + 1, :] = (row & 63).astype(F32)
    src_rows[64:128, :] = jnp.zeros((64, 128), F32)
    src_cols = src_rows[...].T.astype(BF16)
    lane_sq = iota((128, 128), 1)
    sub_sq = iota((128, 128), 0)
    lane_f = lane_sq.astype(F32)
    ones_sq = jnp.ones((128, 128), BF16)
    asks = 8

    def ask(step, _):
        base = step * asks
        pick = (iota((128, asks * 128), 0) == base + iota((128, asks * 128), 1) // 128)
        src_b = dot(src_cols, pick.astype(BF16))
        cols = [src_b[:, j * 128 : j * 128 + 128] for j in range(asks)]
        earlier = []
        for j in range(asks):
            row = src_rows[pl.ds(base + j, 1), :]
            hit = jnp.logical_and(cols[j] == row, lane_sq < sub_sq)
            earlier.append(jnp.where(hit, 1.0, 0.0).astype(BF16))
        slot_b = dot(jnp.concatenate(earlier, axis=0), ones_sq)
        for j in range(asks):
            code = cols[j] + 64.0 * slot_b[j * 128 : j * 128 + 128]
            g2 = jnp.where(code == lane_f, 1.0, 0.0).astype(BF16)
            g2_buf[base + j] = g2
            loc = jnp.broadcast_to(loc_rows[pl.ds(base + j, 1), :], (16, 128)).astype(BF16)
            loc_mat[pl.ds(base + j, 1), :] = dot(loc, g2)[0:1, :]
        return 0

    lax.fori_loop(0, NPAIR // asks, ask, 0)

    loc_cols = loc_mat[...].astype(BF16)

    def choose(s, _):
        pick = iota((128, 256), 0) == s + iota((128, 256), 1) // 128 * 64
        loc_b = dot(loc_cols, pick.astype(BF16))
        loc_b = 2.0 * jnp.concatenate([loc_b[:, 0:128], loc_b[:, 128:256]], axis=0)
        g1_buf[s, :, 0:128] = jnp.where(loc_b == lane_f, 1.0, 0.0).astype(BF16)
        g1_buf[s, :, 128:256] = jnp.where(loc_b + 1.0 == lane_f, 1.0, 0.0).astype(BF16)
        return 0

    lax.fori_loop(0, NPAIR, choose, 0, unroll=4)

    landed(id_buf.at[pl.ds(0, NPAIR - GROUP)], id_sem.at[3]).wait()
    for q in range(32):
        row = id_buf[2 * q] + id_buf[2 * q + 1]
        hit = iota((512, 128), 0) == row
        s_buf[:, q * 128 : q * 128 + 128] = jnp.where(hit, 1.0, 0.0).astype(BF16)

    zero = jnp.zeros((16, 128), BF16)

    batch = 4

    def take(step, _):
        first = step * batch
        sources = [lax.rem(me + NPAIR - offset(first + j), NPAIR) for j in range(batch)]
        for j, s in enumerate(sources):
            if j == 0:

                @pl.when(first > 0)
                def _():
                    landed(recv_buf.at[s], recv_sem.at[s]).wait()

            else:
                landed(recv_buf.at[s], recv_sem.at[s]).wait()
        for s in sources:
            rows = []
            for ri in range(2):
                for ch in range(2):
                    for g in range(2):
                        at = (2 * g + ri) * 16
                        piece = recv_buf[s, at : at + 16, :]
                        halves = [piece, zero] if ch == 0 else [zero, piece]
                        rows.append(jnp.concatenate(halves, axis=1))
            rows_buf[pl.ds(s * STEP, 128), :] = dot_nt(
                g1_buf[s], jnp.concatenate(rows, axis=0)
            )
        return 0

    lax.fori_loop(0, NPAIR // batch, take, 0)

    def cross(p, _):
        asked = [rows_buf[pl.ds(p + 64 * j, 64, stride=STEP), :] for j in range(2)]
        asked = jnp.concatenate(asked, axis=0).astype(BF16)
        sides = dot(g2_buf[p], asked)
        left, right = sides[0:64], sides[64:128]
        to = pl.ds(pl.multiple_of(p * 64, 64), 64)
        p_buf[to, 0:128] = (left * right).astype(BF16)
        p_buf[to, 128:256] = (left * pltpu.roll(right, 64, 1)).astype(BF16)
        return 0

    lax.fori_loop(0, NPAIR, cross, 0, unroll=8)

    seg = (iota((1, 256), 1) >> 4) & 1
    weight = jnp.where(seg == 0, valid_smem[0], valid_smem[1]).astype(F32)
    z = dot(s_buf[...], p_buf[...]) * weight
    high = z.astype(BF16)
    rest = (z - high.astype(F32)).astype(BF16)
    total = jnp.zeros((128, 128), F32)
    for q in range(4):
        fold = fold_ref[q * 256 : q * 256 + 256, :]
        part = slice(q * 128, q * 128 + 128)
        total = total + (dot(high[part], fold) + dot(rest[part], fold))
    for d in range(NPAIR):
        part_buf[d] = total[2 * d : 2 * d + 2, :]

    def send_part(n, _):
        d = lax.rem(me + offset(n), NPAIR)
        remote(part_buf.at[d], got_buf.at[me], (part_sem.at[0], part_sem.at[1]), (tm, d)).start()
        return 0

    lax.fori_loop(1, NPAIR, send_part, 0)
    got_buf[me] = part_buf[me]
    landed(got_buf.at[pl.ds(0, NPAIR - 1)], part_sem.at[1]).wait()

    sub8, lane8 = iota((8, 128), 0), iota((8, 128), 1)
    def spread(tile):
        made = jnp.zeros((8, 128), F32)
        for j in range(4):
            d = 4 * tile + j
            two = got_buf[d]
            both = jnp.where(
                sub8 < 4,
                jnp.broadcast_to(two[0:1, :], (8, 128)),
                jnp.broadcast_to(two[1:2, :], (8, 128)),
            )
            for q in range(4):
                turned = pltpu.roll(both, (32 * (j - q)) % 128, 1) if j != q else both
                fits = jnp.logical_and(sub8 % 4 == q, lane8 // 32 == j)
                made = jnp.where(fits, turned, made)
        return made

    for tile in range(8):
        both = jnp.concatenate([spread(tile), spread(tile + 8)], axis=0)
        spec_buf[tm, :, tile * 128 : tile * 128 + 128] = both.astype(BF16)

    own_spec = spec_buf.at[tm]
    for i in range(1, NTM):
        remote(own_spec, own_spec, (x_sem.at[0], x_sem.at[1]), (lax.rem(tm + i, NTM), me)).start()
    inv_load.wait()
    landed(spec_buf.at[pl.ds(0, NTM - 1)], x_sem.at[1]).wait()
    planes = [spec_buf[i].astype(F32) for i in range(NTM)]
    spec = (planes[0] + planes[1]) + (planes[2] + planes[3])
    high = spec.astype(BF16)
    rest = (spec - high.astype(F32)).astype(BF16)
    lags = dot(jnp.concatenate([high[0:8], rest[0:8]], axis=0), inv_buf[0:1024, :])
    lags = lags + dot(jnp.concatenate([high[8:16], rest[8:16]], axis=0), inv_buf[1024:2048, :])
    out_ref[...] = lags

    landed(send_buf.at[pl.ds(0, NPAIR - 1)], send_sem).wait()
    landed(id_buf.at[pl.ds(0, GROUP - 1)], id_sem.at[0]).wait()
    landed(id_buf.at[pl.ds(0, NPAIR - GROUP)], id_sem.at[2]).wait()
    landed(part_buf.at[pl.ds(0, NPAIR - 1)], part_sem.at[0]).wait()
    landed(spec_buf.at[pl.ds(0, NTM - 1)], x_sem.at[0]).wait()


def on_device(strain, pair_list, pair_bins, bin_slots, seg_valid):
    vmem = pl.BlockSpec(memory_space=pltpu.VMEM)
    smem = pl.BlockSpec(memory_space=pltpu.SMEM)
    hbm = pl.BlockSpec(memory_space=pl.ANY)
    dma = pltpu.SemaphoreType.DMA
    both = pl.pallas_call(
        body,
        out_shape=jax.ShapeDtypeStruct((16, LAGS // NTM), F32),
        in_specs=[hbm, hbm, hbm, vmem, vmem, smem, smem, smem],
        out_specs=vmem,
        scratch_shapes=[
            pltpu.VMEM((2, 128, SEG_LEN), BF16),
            pltpu.VMEM((4, 512, 2 * SUB), BF16),
            pltpu.VMEM((2 * BAND, LAGS // NTM), BF16),
            pltpu.VMEM((4, 256, 2 * SUB), BF16),
            pltpu.VMEM((4, 512, 256), F32),
            pltpu.VMEM((NPAIR, 64, 128), BF16),
            pltpu.VMEM((NPAIR, 64, 128), BF16),
            pltpu.VMEM((NPAIR, 1, 128), jnp.int32),
            pltpu.VMEM((128, 128), F32),
            pltpu.VMEM((64, 128), F32),
            pltpu.VMEM((64, 128), F32),
            pltpu.VMEM((NPAIR, 128, 256), BF16),
            pltpu.VMEM((NPAIR, 128, 128), BF16),
            pltpu.VMEM((512, 4096), BF16),
            pltpu.VMEM((NPAIR * STEP, 128), F32),
            pltpu.VMEM((4096, 256), BF16),
            pltpu.VMEM((NPAIR, 2, 128), F32),
            pltpu.VMEM((NPAIR, 2, 128), F32),
            pltpu.VMEM((NTM, 16, BAND), BF16),
            dma((7,)), dma, dma((NPAIR,)), dma((4,)), dma((2,)), dma((2,)),
        ],
        compiler_params=pltpu.CompilerParams(
            collective_id=0, has_side_effects=True, vmem_limit_bytes=60 << 20
        ),
    )(
        strain,
        jnp.asarray(forward_tables()),
        jnp.asarray(inverse_tables()),
        jnp.asarray(fold_table()),
        pair_list.T,
        pair_bins,
        bin_slots,
        seg_valid,
    )
    return both[0:8] + both[8:16]


def solution(mesh):
    return jax.shard_map(
        on_device,
        mesh=mesh,
        in_specs=(P("tm", "pair", None), P(), P("pair"), P(), P("tm")),
        out_specs=P("pair", "tm"),
        check_vma=False,
    )
```

```python
import functools
import math

import jax
import jax.numpy as jnp
import numpy as np
from jax import lax
from jax.experimental import pallas as pl
from jax.experimental.pallas import tpu as pltpu
from jax.sharding import PartitionSpec as P

SEG_LEN = 8192
BAND = 1024
FIRST_BIN = 128
LAGS = 2048
EPS = 1e-06
NPAIR = 64
NTM = 4
STEP = 129
ID_STEP = 32
GROUP = 8
SUB = SEG_LEN // 8
MESH = pl.DeviceIdType.MESH
F32 = jnp.float32
BF16 = jnp.bfloat16


def owned_bins():
    bins = np.zeros((4, 16, 2, 8), np.int64)
    for c in range(4):
        for a in range(2):
            k1 = (0, 4)[a] if c == 0 else (c, 8 - c)[a]
            for w in range(16):
                bins[c, w, a] = k1 + 8 * (16 + 8 * w + np.arange(8))
    return bins


def forward_tables():
    bins = owned_bins()
    t = np.arange(SUB, dtype=np.int64)
    theta = (bins[..., None] * t % SEG_LEN) * (2.0 * math.pi / SEG_LEN)
    cos, sin = np.cos(theta), np.sin(theta)
    table = np.zeros((4, 16, 2, 2, 8, 2, SUB), np.float64)
    sign = (1.0, -1.0)
    for c in range(4):
        for a in range(2):
            if c == 0:
                table[c, :, 0, a, :, a] = cos[c, :, a]
                table[c, :, 1, a, :, a] = -sin[c, :, a]
            else:
                table[c, :, 0, a, :, 0] = cos[c, :, a]
                table[c, :, 0, a, :, 1] = sign[a] * sin[c, :, a]
                table[c, :, 1, a, :, 0] = -sin[c, :, a]
                table[c, :, 1, a, :, 1] = sign[a] * cos[c, :, a]
    first = np.stack([table[0, :, :, a, :, a] for a in range(2)])
    rest = table[1:].reshape(3, 512, 2 * SUB)
    return first.reshape(512, SUB).astype(jnp.bfloat16), rest.astype(jnp.bfloat16)


def inverse_tables():
    bins = owned_bins().reshape(NPAIR, 16)
    lag = np.arange(LAGS, dtype=np.int64) - LAGS // 2
    phi = (bins[..., None] * lag % SEG_LEN) * (2.0 * math.pi / SEG_LEN)
    factor = 1.0 / math.sqrt(BAND)
    table = np.stack([np.cos(phi) * factor, -np.sin(phi) * factor], axis=1)
    table = table.reshape(2 * BAND, NTM, LAGS // NTM).transpose(1, 0, 2)
    return np.ascontiguousarray(table).astype(jnp.bfloat16)


def fold_table():
    table = np.zeros((4, 2, 2, 2, 2, 16, 4, 2, 16), np.float32)
    for q in range(4):
        for b in range(16):
            table[q, 0, 0, :, :, b, q, 0, b] = 1.0
            table[q, 0, 1, :, :, b, q, 0, b] = 1.0
            table[q, 1, 0, :, :, b, q, 1, b] = -1.0
            table[q, 1, 1, :, :, b, q, 1, b] = 1.0
    return table.reshape(1024, 128).astype(jnp.bfloat16)


def iota(shape, dim):
    return lax.broadcasted_iota(jnp.int32, shape, dim)


def dot(a, b):
    return jnp.dot(a, b, preferred_element_type=F32)


def dot_nt(a, b):
    return lax.dot_general(a, b, (((1,), (1,)), ((), ())), preferred_element_type=F32)


def body(
    x_hbm, real_hbm, tab_hbm, inv_hbm, fold_hbm, pairs_hbm, bins_smem, slots_smem, valid_smem,
    out_ref,
    x_buf, real_buf, tab_buf, inv_buf, fold_ref, pairs_ref, y_buf, r_buf, send_buf, recv_buf, id_buf,
    src_rows, loc_rows, loc_mat, g1_buf, g2_buf, s_buf, rows_buf, p_buf,
    part_buf, got_buf, spec_buf,
    load_sem, send_sem, recv_sem, id_sem, part_sem, x_sem,
):
    tm = lax.axis_index("tm")
    me = lax.axis_index("pair")

    def x_load(n):
        rows = pl.ds(n % 2 * 64, 64)
        return pltpu.make_async_copy(x_hbm.at[n // 2, rows], x_buf.at[n // 2, rows], load_sem.at[n])

    def tab_load(c):
        if c == 0:
            return pltpu.make_async_copy(real_hbm, real_buf, load_sem.at[4])
        return pltpu.make_async_copy(tab_hbm.at[c - 1], tab_buf.at[c - 1], load_sem.at[4 + c])

    inv_load = pltpu.make_async_copy(inv_hbm.at[tm], inv_buf, load_sem.at[8])
    fold_load = pltpu.make_async_copy(fold_hbm, fold_ref, load_sem.at[9])
    pairs_load = pltpu.make_async_copy(pairs_hbm, pairs_ref, load_sem.at[10])
    for n in range(4):
        x_load(n).start()
    for c in range(4):
        tab_load(c).start()
    pairs_load.start()
    inv_load.start()
    fold_load.start()

    barrier = pltpu.get_barrier_semaphore()

    def greet(i):
        pl.semaphore_signal(barrier, inc=1, device_id=(tm, lax.rem(me + i, NPAIR)), device_id_type=MESH)

    for i in range(1, 8):
        greet(i)
    for i in range(1, NTM):
        pl.semaphore_signal(barrier, inc=1, device_id=(lax.rem(tm + i, NTM), me), device_id_type=MESH)

    lane = iota((1, 128), 1)
    first_lane = lax.rem(me, 2) * 64

    def one_id(k, row):
        r = slots_smem[bins_smem[k]]
        code = (r & 3) * 128 + (r >> 3) * 2 + ((r >> 2) & 1)
        return jnp.where(lane == first_lane + k, code, row)

    id_buf[me] = lax.fori_loop(0, 64, one_id, jnp.zeros((1, 128), jnp.int32))

    root = math.sqrt(0.5)
    greeted = (8, 24, 40, 52)
    for n in range(4):
        x_load(n).wait()

        def split(step, _, n=n):
            s, some = n // 2, (4, 4, 3, 3)[n]
            for j in range(some):
                greet(greeted[n] + step * some + j)
            rows = pl.ds(pl.multiple_of(n % 2 * 64 + step * 16, 16), 16)
            to = pl.ds(pl.multiple_of(n * 64 + step * 16, 16), 16)
            for h in range(2):
                v = [
                    x_buf[s, rows, e * SUB + h * 512 : e * SUB + h * 512 + 512].astype(F32)
                    for e in range(8)
                ]
                s04, s26, s15, s37 = v[0] + v[4], v[2] + v[6], v[1] + v[5], v[3] + v[7]
                d04, d26, d15, d37 = v[0] - v[4], v[2] - v[6], v[1] - v[5], v[3] - v[7]
                even, odd = s04 + s26, s15 + s37
                diff, both = (d15 - d37) * root, (d15 + d37) * root
                parts = (
                    (even + odd, even - odd),
                    (d04 + diff, -d26 - both),
                    (s04 - s26, s37 - s15),
                    (d04 - diff, d26 - both),
                )
                for c in range(4):
                    for part in range(2):
                        at = part * SUB + h * 512
                        y_buf[c, to, at : at + 512] = parts[c][part].astype(BF16)
            return 0

        lax.fori_loop(0, 4, split, 0)

    here = me // GROUP * GROUP
    mine = lax.rem(me, GROUP)

    def remote(src, dst, sems, to):
        return pltpu.make_async_remote_copy(
            src_ref=src, dst_ref=dst, send_sem=sems[0], recv_sem=sems[1],
            device_id=to, device_id_type=MESH,
        )

    def landed(ref, sem):
        return pltpu.make_async_copy(ref, ref, sem)

    def offset(n):
        return (32 + n // 2 * (1 - n % 2 * 2)) * jnp.minimum(n, 1)

    for c in range(4):
        tab_load(c).wait()
        if c == 0:
            r_buf[0, 0:256] = dot_nt(real_buf[0:256], y_buf[0, :, 0:SUB])
            r_buf[0, 256:512] = dot_nt(real_buf[256:512], y_buf[0, :, SUB : 2 * SUB])
        else:
            r_buf[c] = dot_nt(tab_buf[c - 1], y_buf[c])

    def white(w):
        rows = pl.ds(pl.multiple_of(w * 32, 32), 32)
        both = [r_buf[0, pl.ds(pl.multiple_of(a * 256 + w * 16, 16), 16), :] for a in range(2)]
        real = jnp.concatenate([both[0][0:8], both[1][0:8], both[0][8:16], both[1][8:16]], axis=0)
        parts = [real] + [r_buf[c, rows, :] for c in range(1, 4)]
        power = parts[0] * parts[0]
        for c in range(1, 4):
            power = power + parts[c] * parts[c]
        energy = jnp.sum(power, axis=0, keepdims=True) * (1.0 / 64.0)
        scale = lax.rsqrt(energy + EPS)
        for c in range(4):
            done = (parts[c] * scale).astype(BF16)
            send_buf[c * 16 + w, 0:32, :] = done[:, 0:128]
            send_buf[c * 16 + w, 32:64, :] = done[:, 128:256]

    def white_step(w, _):
        white(w)
        return 0

    lax.fori_loop(0, 16, white_step, 0, unroll=8)

    pl.semaphore_wait(barrier, NPAIR - 1 + NTM - 1)

    for i in range(1, GROUP):
        to = here + lax.rem(mine + i, GROUP)
        remote(id_buf.at[me], id_buf.at[me], (id_sem.at[0], id_sem.at[1]), (tm, to)).start()

    def send_main(n, _):
        d = lax.rem(me + offset(n), NPAIR)
        remote(send_buf.at[d], recv_buf.at[me], (send_sem, recv_sem.at[me]), (tm, d)).start()
        return 0

    lax.fori_loop(1, ID_STEP, send_main, 0)
    landed(id_buf.at[pl.ds(0, GROUP - 1)], id_sem.at[1]).wait()
    own_group = id_buf.at[pl.ds(here, GROUP)]
    for i in range(1, GROUP):
        to = lax.rem(me + i * GROUP, NPAIR)
        remote(own_group, own_group, (id_sem.at[2], id_sem.at[3]), (tm, to)).start()
    lax.fori_loop(ID_STEP, NPAIR, send_main, 0)
    recv_buf[me] = send_buf[me]
    pairs_load.wait()

    low = iota((1, 128), 1) < 64
    for q in range(32):
        a = pairs_ref[0:1, q * 128 : q * 128 + 128]
        b = pairs_ref[1:2, q * 128 : q * 128 + 128]
        first = jnp.where(low, a, pltpu.roll(b, 64, 1))
        second = jnp.where(low, pltpu.roll(a, 64, 1), b)
        for j, row in enumerate((first, second)):
            src_rows[2 * q + j : 2 * q + j + 1, :] = (row >> 6).astype(F32)
            loc_rows[2 * q + j : 2 * q + j + 1, :] = (row & 63).astype(F32)
    src_rows[64:128, :] = jnp.zeros((64, 128), F32)
    src_cols = src_rows[...].T.astype(BF16)
    lane_sq = iota((128, 128), 1)
    sub_sq = iota((128, 128), 0)
    lane_f = lane_sq.astype(F32)
    ones_sq = jnp.ones((128, 128), BF16)
    asks = 8

    def ask(step, _):
        base = step * asks
        pick = (iota((128, asks * 128), 0) == base + iota((128, asks * 128), 1) // 128)
        src_b = dot(src_cols, pick.astype(BF16))
        cols = [src_b[:, j * 128 : j * 128 + 128] for j in range(asks)]
        earlier = []
        for j in range(asks):
            row = src_rows[pl.ds(base + j, 1), :]
            hit = jnp.logical_and(cols[j] == row, lane_sq < sub_sq)
            earlier.append(jnp.where(hit, 1.0, 0.0).astype(BF16))
        slot_b = dot(jnp.concatenate(earlier, axis=0), ones_sq)
        for j in range(asks):
            code = cols[j] + 64.0 * slot_b[j * 128 : j * 128 + 128]
            g2 = jnp.where(code == lane_f, 1.0, 0.0).astype(BF16)
            g2_buf[base + j] = g2
            loc = jnp.broadcast_to(loc_rows[pl.ds(base + j, 1), :], (16, 128)).astype(BF16)
            loc_mat[pl.ds(base + j, 1), :] = dot(loc, g2)[0:1, :]
        return 0

    lax.fori_loop(0, NPAIR // asks, ask, 0)

    loc_cols = loc_mat[...].astype(BF16)

    def choose(s, _):
        pick = iota((128, 256), 0) == s + iota((128, 256), 1) // 128 * 64
        loc_b = dot(loc_cols, pick.astype(BF16))
        loc_b = 2.0 * jnp.concatenate([loc_b[:, 0:128], loc_b[:, 128:256]], axis=0)
        g1_buf[s, :, 0:128] = jnp.where(loc_b == lane_f, 1.0, 0.0).astype(BF16)
        g1_buf[s, :, 128:256] = jnp.where(loc_b + 1.0 == lane_f, 1.0, 0.0).astype(BF16)
        return 0

    lax.fori_loop(0, NPAIR, choose, 0, unroll=4)

    landed(id_buf.at[pl.ds(0, NPAIR - GROUP)], id_sem.at[3]).wait()
    for q in range(32):
        row = id_buf[2 * q] + id_buf[2 * q + 1]
        hit = iota((512, 128), 0) == row
        s_buf[:, q * 128 : q * 128 + 128] = jnp.where(hit, 1.0, 0.0).astype(BF16)

    zero = jnp.zeros((16, 128), BF16)

    batch = 4

    def take(step, _):
        first = step * batch
        sources = [lax.rem(me + NPAIR - offset(first + j), NPAIR) for j in range(batch)]

        @pl.when(first > 0)
        def _():
            landed(recv_buf.at[sources[0]], recv_sem.at[sources[0]]).wait()

        for s in sources[1:]:
            landed(recv_buf.at[s], recv_sem.at[s]).wait()
        for s in sources:
            rows = []
            for ri in range(2):
                for ch in range(2):
                    for g in range(2):
                        at = (2 * g + ri) * 16
                        piece = recv_buf[s, at : at + 16, :]
                        halves = [piece, zero] if ch == 0 else [zero, piece]
                        rows.append(jnp.concatenate(halves, axis=1))
            rows_buf[pl.ds(s * STEP, 128), :] = dot_nt(
                g1_buf[s], jnp.concatenate(rows, axis=0)
            )
        return 0

    lax.fori_loop(0, 16, take, 0)

    def cross(p, _):
        asked = [rows_buf[pl.ds(p + 64 * j, 64, stride=STEP), :] for j in range(2)]
        asked = jnp.concatenate(asked, axis=0).astype(BF16)
        sides = dot(g2_buf[p], asked)
        left, right = sides[0:64], sides[64:128]
        to = pl.ds(pl.multiple_of(p * 64, 64), 64)
        p_buf[to, 0:128] = (left * right).astype(BF16)
        p_buf[to, 128:256] = (left * pltpu.roll(right, 64, 1)).astype(BF16)
        return 0

    lax.fori_loop(0, NPAIR, cross, 0, unroll=8)

    seg = (iota((1, 256), 1) >> 4) & 1
    weight = jnp.where(seg == 0, valid_smem[0], valid_smem[1]).astype(F32)
    fold_load.wait()
    z = dot(s_buf[...], p_buf[...]) * weight
    high = z.astype(BF16)
    rest = (z - high.astype(F32)).astype(BF16)
    total = jnp.zeros((128, 128), F32)
    for q in range(4):
        fold = fold_ref[q * 256 : q * 256 + 256, :]
        part = slice(q * 128, q * 128 + 128)
        total = total + (dot(high[part], fold) + dot(rest[part], fold))
    for d in range(NPAIR):
        part_buf[d] = total[2 * d : 2 * d + 2, :]

    def send_part(n, _):
        d = lax.rem(me + offset(n), NPAIR)
        remote(part_buf.at[d], got_buf.at[me], (part_sem.at[0], part_sem.at[1]), (tm, d)).start()
        return 0

    lax.fori_loop(1, NPAIR, send_part, 0)
    got_buf[me] = part_buf[me]
    landed(got_buf.at[pl.ds(0, NPAIR - 1)], part_sem.at[1]).wait()

    sub8, lane8 = iota((8, 128), 0), iota((8, 128), 1)
    def spread(tile):
        made = jnp.zeros((8, 128), F32)
        for j in range(4):
            d = 4 * tile + j
            two = got_buf[d]
            both = jnp.where(
                sub8 < 4,
                jnp.broadcast_to(two[0:1, :], (8, 128)),
                jnp.broadcast_to(two[1:2, :], (8, 128)),
            )
            for q in range(4):
                turned = pltpu.roll(both, (32 * (j - q)) % 128, 1) if j != q else both
                fits = jnp.logical_and(sub8 % 4 == q, lane8 // 32 == j)
                made = jnp.where(fits, turned, made)
        return made

    for tile in range(8):
        both = jnp.concatenate([spread(tile), spread(tile + 8)], axis=0)
        spec_buf[tm, :, tile * 128 : tile * 128 + 128] = both.astype(BF16)

    own_spec = spec_buf.at[tm]
    for i in range(1, NTM):
        remote(own_spec, own_spec, (x_sem.at[0], x_sem.at[1]), (lax.rem(tm + i, NTM), me)).start()
    inv_load.wait()
    landed(spec_buf.at[pl.ds(0, NTM - 1)], x_sem.at[1]).wait()
    planes = [spec_buf[i].astype(F32) for i in range(NTM)]
    spec = (planes[0] + planes[1]) + (planes[2] + planes[3])
    high = spec.astype(BF16)
    rest = (spec - high.astype(F32)).astype(BF16)
    lags = dot(jnp.concatenate([high[0:8], rest[0:8]], axis=0), inv_buf[0:1024, :])
    lags = lags + dot(jnp.concatenate([high[8:16], rest[8:16]], axis=0), inv_buf[1024:2048, :])
    out_ref[...] = lags

    landed(send_buf.at[pl.ds(0, NPAIR - 1)], send_sem).wait()
    landed(id_buf.at[pl.ds(0, GROUP - 1)], id_sem.at[0]).wait()
    landed(id_buf.at[pl.ds(0, NPAIR - GROUP)], id_sem.at[2]).wait()
    landed(part_buf.at[pl.ds(0, NPAIR - 1)], part_sem.at[0]).wait()
    landed(spec_buf.at[pl.ds(0, NTM - 1)], x_sem.at[0]).wait()


def on_device(strain, pair_list, pair_bins, bin_slots, seg_valid):
    vmem = pl.BlockSpec(memory_space=pltpu.VMEM)
    smem = pl.BlockSpec(memory_space=pltpu.SMEM)
    hbm = pl.BlockSpec(memory_space=pl.ANY)
    dma = pltpu.SemaphoreType.DMA
    both = pl.pallas_call(
        body,
        out_shape=jax.ShapeDtypeStruct((16, LAGS // NTM), F32),
        in_specs=[hbm, hbm, hbm, hbm, hbm, hbm, smem, smem, smem],
        out_specs=vmem,
        scratch_shapes=[
            pltpu.VMEM((2, 128, SEG_LEN), BF16),
            pltpu.VMEM((512, SUB), BF16),
            pltpu.VMEM((3, 512, 2 * SUB), BF16),
            pltpu.VMEM((2 * BAND, LAGS // NTM), BF16),
            pltpu.VMEM((1024, 128), BF16),
            pltpu.VMEM((2, 4096), jnp.int32),
            pltpu.VMEM((4, 256, 2 * SUB), BF16),
            pltpu.VMEM((4, 512, 256), F32),
            pltpu.VMEM((NPAIR, 64, 128), BF16),
            pltpu.VMEM((NPAIR, 64, 128), BF16),
            pltpu.VMEM((NPAIR, 1, 128), jnp.int32),
            pltpu.VMEM((128, 128), F32),
            pltpu.VMEM((64, 128), F32),
            pltpu.VMEM((64, 128), F32),
            pltpu.VMEM((NPAIR, 128, 256), BF16),
            pltpu.VMEM((NPAIR, 128, 128), BF16),
            pltpu.VMEM((512, 4096), BF16),
            pltpu.VMEM((NPAIR * STEP, 128), F32),
            pltpu.VMEM((4096, 256), BF16),
            pltpu.VMEM((NPAIR, 2, 128), F32),
            pltpu.VMEM((NPAIR, 2, 128), F32),
            pltpu.VMEM((NTM, 16, BAND), BF16),
            dma((11,)), dma, dma((NPAIR,)), dma((4,)), dma((2,)), dma((2,)),
        ],
        compiler_params=pltpu.CompilerParams(
            collective_id=0, has_side_effects=True, vmem_limit_bytes=60 << 20
        ),
    )(
        strain,
        *(jnp.asarray(table) for table in forward_tables()),
        jnp.asarray(inverse_tables()),
        jnp.asarray(fold_table()),
        pair_list.T,
        pair_bins,
        bin_slots,
        seg_valid,
    )
    return both[0:8] + both[8:16]


def solution(mesh):
    return jax.shard_map(
        on_device,
        mesh=mesh,
        in_specs=(P("tm", "pair", None), P(), P("pair"), P(), P("tm")),
        out_specs=P("pair", "tm"),
        check_vma=False,
    )
```

```python
import functools
import math

import jax
import jax.numpy as jnp
import numpy as np
from jax import lax
from jax.experimental import pallas as pl
from jax.experimental.pallas import tpu as pltpu
from jax.sharding import PartitionSpec as P

SEG_LEN = 8192
BAND = 1024
FIRST_BIN = 128
LAGS = 2048
EPS = 1e-06
NPAIR = 64
NTM = 4
STEP = 129
ID_STEP = 16
GROUP = 8
SUB = SEG_LEN // 8
MESH = pl.DeviceIdType.MESH
F32 = jnp.float32
BF16 = jnp.bfloat16


def owned_bins():
    bins = np.zeros((4, 16, 2, 8), np.int64)
    for c in range(4):
        for a in range(2):
            k1 = (0, 4)[a] if c == 0 else (c, 8 - c)[a]
            for w in range(16):
                bins[c, w, a] = k1 + 8 * (16 + 8 * w + np.arange(8))
    return bins


def forward_tables():
    bins = owned_bins()
    t = np.arange(SUB, dtype=np.int64)
    theta = (bins[..., None] * t % SEG_LEN) * (2.0 * math.pi / SEG_LEN)
    cos, sin = np.cos(theta), np.sin(theta)
    table = np.zeros((4, 16, 2, 2, 8, 2, SUB), np.float64)
    sign = (1.0, -1.0)
    for c in range(4):
        for a in range(2):
            if c == 0:
                table[c, :, 0, a, :, a] = cos[c, :, a]
                table[c, :, 1, a, :, a] = -sin[c, :, a]
            else:
                table[c, :, 0, a, :, 0] = cos[c, :, a]
                table[c, :, 0, a, :, 1] = sign[a] * sin[c, :, a]
                table[c, :, 1, a, :, 0] = -sin[c, :, a]
                table[c, :, 1, a, :, 1] = sign[a] * cos[c, :, a]
    first = np.stack([table[0, :, :, a, :, a] for a in range(2)])
    rest = table[1:].reshape(3, 512, 2 * SUB)
    return first.reshape(512, SUB).astype(jnp.bfloat16), rest.astype(jnp.bfloat16)


def inverse_tables():
    bins = owned_bins().reshape(NPAIR, 16)
    lag = np.arange(LAGS, dtype=np.int64) - LAGS // 2
    phi = (bins[..., None] * lag % SEG_LEN) * (2.0 * math.pi / SEG_LEN)
    factor = 1.0 / math.sqrt(BAND)
    table = np.stack([np.cos(phi) * factor, -np.sin(phi) * factor], axis=1)
    table = table.reshape(2 * BAND, NTM, LAGS // NTM).transpose(1, 0, 2)
    return np.ascontiguousarray(table).astype(jnp.bfloat16)


def fold_table():
    table = np.zeros((4, 2, 2, 2, 2, 16, 4, 2, 16), np.float32)
    for q in range(4):
        for b in range(16):
            table[q, 0, 0, :, :, b, q, 0, b] = 1.0
            table[q, 0, 1, :, :, b, q, 0, b] = 1.0
            table[q, 1, 0, :, :, b, q, 1, b] = -1.0
            table[q, 1, 1, :, :, b, q, 1, b] = 1.0
    return table.reshape(1024, 128).astype(jnp.bfloat16)


def iota(shape, dim):
    return lax.broadcasted_iota(jnp.int32, shape, dim)


def dot(a, b):
    return jnp.dot(a, b, preferred_element_type=F32)


def dot_nt(a, b):
    return lax.dot_general(a, b, (((1,), (1,)), ((), ())), preferred_element_type=F32)


def body(
    x_hbm, real_hbm, tab_hbm, inv_hbm, fold_hbm, pairs_hbm, bins_smem, slots_smem, valid_smem,
    out_ref,
    x_buf, real_buf, tab_buf, inv_buf, fold_ref, pairs_ref, y_buf, r_buf, send_buf, recv_buf, id_buf,
    src_rows, loc_rows, loc_mat, g1_buf, g2_buf, s_buf, rows_buf, p_buf,
    part_buf, got_buf, spec_buf,
    load_sem, send_sem, recv_sem, id_sem, part_sem, x_sem,
):
    tm = lax.axis_index("tm")
    me = lax.axis_index("pair")

    def x_load(n):
        rows = pl.ds(n % 2 * 64, 64)
        return pltpu.make_async_copy(x_hbm.at[n // 2, rows], x_buf.at[n // 2, rows], load_sem.at[n])

    def tab_load(c):
        if c == 0:
            return pltpu.make_async_copy(real_hbm, real_buf, load_sem.at[4])
        return pltpu.make_async_copy(tab_hbm.at[c - 1], tab_buf.at[c - 1], load_sem.at[4 + c])

    inv_load = pltpu.make_async_copy(inv_hbm.at[tm], inv_buf, load_sem.at[8])
    fold_load = pltpu.make_async_copy(fold_hbm, fold_ref, load_sem.at[9])
    pairs_load = pltpu.make_async_copy(pairs_hbm, pairs_ref, load_sem.at[10])
    for n in range(4):
        x_load(n).start()
    for c in range(4):
        tab_load(c).start()
    pairs_load.start()
    inv_load.start()
    fold_load.start()

    barrier = pltpu.get_barrier_semaphore()

    def greet(i):
        pl.semaphore_signal(barrier, inc=1, device_id=(tm, lax.rem(me + i, NPAIR)), device_id_type=MESH)

    for i in range(1, 8):
        greet(i)
    for i in range(1, NTM):
        pl.semaphore_signal(barrier, inc=1, device_id=(lax.rem(tm + i, NTM), me), device_id_type=MESH)

    lane = iota((1, 128), 1)
    first_lane = lax.rem(me, 2) * 64

    def one_id(k, row):
        r = slots_smem[bins_smem[k]]
        code = (r & 3) * 128 + (r >> 3) * 2 + ((r >> 2) & 1)
        return jnp.where(lane == first_lane + k, code, row)

    id_buf[me] = lax.fori_loop(0, 64, one_id, jnp.zeros((1, 128), jnp.int32))

    root = math.sqrt(0.5)
    greeted = (8, 24, 40, 52)
    for n in range(4):
        x_load(n).wait()

        def split(step, _, n=n):
            s, some = n // 2, (4, 4, 3, 3)[n]
            for j in range(some):
                greet(greeted[n] + step * some + j)
            rows = pl.ds(pl.multiple_of(n % 2 * 64 + step * 16, 16), 16)
            to = pl.ds(pl.multiple_of(n * 64 + step * 16, 16), 16)
            for h in range(2):
                v = [
                    x_buf[s, rows, e * SUB + h * 512 : e * SUB + h * 512 + 512].astype(F32)
                    for e in range(8)
                ]
                s04, s26, s15, s37 = v[0] + v[4], v[2] + v[6], v[1] + v[5], v[3] + v[7]
                d04, d26, d15, d37 = v[0] - v[4], v[2] - v[6], v[1] - v[5], v[3] - v[7]
                even, odd = s04 + s26, s15 + s37
                diff, both = (d15 - d37) * root, (d15 + d37) * root
                parts = (
                    (even + odd, even - odd),
                    (d04 + diff, -d26 - both),
                    (s04 - s26, s37 - s15),
                    (d04 - diff, d26 - both),
                )
                for c in range(4):
                    for part in range(2):
                        at = part * SUB + h * 512
                        y_buf[c, to, at : at + 512] = parts[c][part].astype(BF16)
            return 0

        lax.fori_loop(0, 4, split, 0)

    here = me // GROUP * GROUP
    mine = lax.rem(me, GROUP)

    def remote(src, dst, sems, to):
        return pltpu.make_async_remote_copy(
            src_ref=src, dst_ref=dst, send_sem=sems[0], recv_sem=sems[1],
            device_id=to, device_id_type=MESH,
        )

    def landed(ref, sem):
        return pltpu.make_async_copy(ref, ref, sem)

    def offset(n):
        return (32 + n // 2 * (1 - n % 2 * 2)) * jnp.minimum(n, 1)

    for c in range(4):
        tab_load(c).wait()
        if c == 0:
            r_buf[0, 0:256] = dot_nt(real_buf[0:256], y_buf[0, :, 0:SUB])
            r_buf[0, 256:512] = dot_nt(real_buf[256:512], y_buf[0, :, SUB : 2 * SUB])
        else:
            r_buf[c] = dot_nt(tab_buf[c - 1], y_buf[c])

    def white(w):
        rows = pl.ds(pl.multiple_of(w * 32, 32), 32)
        both = [r_buf[0, pl.ds(pl.multiple_of(a * 256 + w * 16, 16), 16), :] for a in range(2)]
        real = jnp.concatenate([both[0][0:8], both[1][0:8], both[0][8:16], both[1][8:16]], axis=0)
        parts = [real] + [r_buf[c, rows, :] for c in range(1, 4)]
        power = parts[0] * parts[0]
        for c in range(1, 4):
            power = power + parts[c] * parts[c]
        energy = jnp.sum(power, axis=0, keepdims=True) * (1.0 / 64.0)
        scale = lax.rsqrt(energy + EPS)
        for c in range(4):
            done = (parts[c] * scale).astype(BF16)
            send_buf[c * 16 + w, 0:32, :] = done[:, 0:128]
            send_buf[c * 16 + w, 32:64, :] = done[:, 128:256]

    def white_step(w, _):
        white(w)
        return 0

    lax.fori_loop(0, 16, white_step, 0, unroll=8)

    pl.semaphore_wait(barrier, NPAIR - 1 + NTM - 1)

    for i in range(1, GROUP):
        to = here + lax.rem(mine + i, GROUP)
        remote(id_buf.at[me], id_buf.at[me], (id_sem.at[0], id_sem.at[1]), (tm, to)).start()

    def send_main(n, _):
        d = lax.rem(me + offset(n), NPAIR)
        remote(send_buf.at[d], recv_buf.at[me], (send_sem, recv_sem.at[me]), (tm, d)).start()
        return 0

    lax.fori_loop(1, ID_STEP, send_main, 0)
    landed(id_buf.at[pl.ds(0, GROUP - 1)], id_sem.at[1]).wait()
    own_group = id_buf.at[pl.ds(here, GROUP)]
    for i in range(1, GROUP):
        to = lax.rem(me + i * GROUP, NPAIR)
        remote(own_group, own_group, (id_sem.at[2], id_sem.at[3]), (tm, to)).start()
    lax.fori_loop(ID_STEP, NPAIR, send_main, 0)
    recv_buf[me] = send_buf[me]
    pairs_load.wait()

    low = iota((1, 128), 1) < 64
    for q in range(32):
        a = pairs_ref[0:1, q * 128 : q * 128 + 128]
        b = pairs_ref[1:2, q * 128 : q * 128 + 128]
        first = jnp.where(low, a, pltpu.roll(b, 64, 1))
        second = jnp.where(low, pltpu.roll(a, 64, 1), b)
        for j, row in enumerate((first, second)):
            src_rows[2 * q + j : 2 * q + j + 1, :] = (row >> 6).astype(F32)
            loc_rows[2 * q + j : 2 * q + j + 1, :] = (row & 63).astype(F32)
    src_rows[64:128, :] = jnp.zeros((64, 128), F32)
    src_cols = src_rows[...].T.astype(BF16)
    lane_sq = iota((128, 128), 1)
    sub_sq = iota((128, 128), 0)
    lane_f = lane_sq.astype(F32)
    ones_sq = jnp.ones((128, 128), BF16)
    asks = 8

    def ask(step, _):
        base = step * asks
        pick = (iota((128, asks * 128), 0) == base + iota((128, asks * 128), 1) // 128)
        src_b = dot(src_cols, pick.astype(BF16))
        cols = [src_b[:, j * 128 : j * 128 + 128] for j in range(asks)]
        earlier = []
        for j in range(asks):
            row = src_rows[pl.ds(base + j, 1), :]
            hit = jnp.logical_and(cols[j] == row, lane_sq < sub_sq)
            earlier.append(jnp.where(hit, 1.0, 0.0).astype(BF16))
        slot_b = dot(jnp.concatenate(earlier, axis=0), ones_sq)
        for j in range(asks):
            code = cols[j] + 64.0 * slot_b[j * 128 : j * 128 + 128]
            g2 = jnp.where(code == lane_f, 1.0, 0.0).astype(BF16)
            g2_buf[base + j] = g2
            loc = jnp.broadcast_to(loc_rows[pl.ds(base + j, 1), :], (16, 128)).astype(BF16)
            loc_mat[pl.ds(base + j, 1), :] = dot(loc, g2)[0:1, :]
        return 0

    lax.fori_loop(0, NPAIR // asks, ask, 0)

    loc_cols = loc_mat[...].astype(BF16)

    def choose(s, _):
        pick = iota((128, 256), 0) == s + iota((128, 256), 1) // 128 * 64
        loc_b = dot(loc_cols, pick.astype(BF16))
        loc_b = 2.0 * jnp.concatenate([loc_b[:, 0:128], loc_b[:, 128:256]], axis=0)
        g1_buf[s, :, 0:128] = jnp.where(loc_b == lane_f, 1.0, 0.0).astype(BF16)
        g1_buf[s, :, 128:256] = jnp.where(loc_b + 1.0 == lane_f, 1.0, 0.0).astype(BF16)
        return 0

    lax.fori_loop(0, NPAIR, choose, 0, unroll=4)

    landed(id_buf.at[pl.ds(0, NPAIR - GROUP)], id_sem.at[3]).wait()
    for q in range(32):
        row = id_buf[2 * q] + id_buf[2 * q + 1]
        hit = iota((512, 128), 0) == row
        s_buf[:, q * 128 : q * 128 + 128] = jnp.where(hit, 1.0, 0.0).astype(BF16)

    zero = jnp.zeros((16, 128), BF16)

    batch = 8

    def take(step, _):
        first = step * batch
        sources = [lax.rem(me + NPAIR - offset(first + j), NPAIR) for j in range(batch)]

        @pl.when(first > 0)
        def _():
            landed(recv_buf.at[sources[0]], recv_sem.at[sources[0]]).wait()

        for s in sources[1:]:
            landed(recv_buf.at[s], recv_sem.at[s]).wait()
        for s in sources:
            rows = []
            for ri in range(2):
                for ch in range(2):
                    for g in range(2):
                        at = (2 * g + ri) * 16
                        piece = recv_buf[s, at : at + 16, :]
                        halves = [piece, zero] if ch == 0 else [zero, piece]
                        rows.append(jnp.concatenate(halves, axis=1))
            rows_buf[pl.ds(s * STEP, 128), :] = dot_nt(
                g1_buf[s], jnp.concatenate(rows, axis=0)
            )
        return 0

    lax.fori_loop(0, NPAIR // batch, take, 0)

    def cross(p, _):
        asked = [rows_buf[pl.ds(p + 64 * j, 64, stride=STEP), :] for j in range(2)]
        asked = jnp.concatenate(asked, axis=0).astype(BF16)
        sides = dot(g2_buf[p], asked)
        left, right = sides[0:64], sides[64:128]
        to = pl.ds(pl.multiple_of(p * 64, 64), 64)
        p_buf[to, 0:128] = (left * right).astype(BF16)
        p_buf[to, 128:256] = (left * pltpu.roll(right, 64, 1)).astype(BF16)
        return 0

    lax.fori_loop(0, NPAIR, cross, 0, unroll=16)

    seg = (iota((1, 256), 1) >> 4) & 1
    weight = jnp.where(seg == 0, valid_smem[0], valid_smem[1]).astype(F32)
    fold_load.wait()
    z = dot(s_buf[...], p_buf[...]) * weight
    high = z.astype(BF16)
    rest = (z - high.astype(F32)).astype(BF16)
    total = jnp.zeros((128, 128), F32)
    for q in range(4):
        fold = fold_ref[q * 256 : q * 256 + 256, :]
        part = slice(q * 128, q * 128 + 128)
        total = total + (dot(high[part], fold) + dot(rest[part], fold))
    for d in range(NPAIR):
        part_buf[d] = total[2 * d : 2 * d + 2, :]

    def send_part(n, _):
        d = lax.rem(me + offset(n), NPAIR)
        remote(part_buf.at[d], got_buf.at[me], (part_sem.at[0], part_sem.at[1]), (tm, d)).start()
        return 0

    lax.fori_loop(1, NPAIR, send_part, 0)
    got_buf[me] = part_buf[me]
    landed(got_buf.at[pl.ds(0, NPAIR - 1)], part_sem.at[1]).wait()

    sub8, lane8 = iota((8, 128), 0), iota((8, 128), 1)
    def spread(tile):
        made = jnp.zeros((8, 128), F32)
        for j in range(4):
            d = 4 * tile + j
            two = got_buf[d]
            both = jnp.where(
                sub8 < 4,
                jnp.broadcast_to(two[0:1, :], (8, 128)),
                jnp.broadcast_to(two[1:2, :], (8, 128)),
            )
            for q in range(4):
                turned = pltpu.roll(both, (32 * (j - q)) % 128, 1) if j != q else both
                fits = jnp.logical_and(sub8 % 4 == q, lane8 // 32 == j)
                made = jnp.where(fits, turned, made)
        return made

    for tile in range(8):
        both = jnp.concatenate([spread(tile), spread(tile + 8)], axis=0)
        spec_buf[tm, :, tile * 128 : tile * 128 + 128] = both.astype(BF16)

    own_spec = spec_buf.at[tm]
    for i in range(1, NTM):
        remote(own_spec, own_spec, (x_sem.at[0], x_sem.at[1]), (lax.rem(tm + i, NTM), me)).start()
    inv_load.wait()
    landed(spec_buf.at[pl.ds(0, NTM - 1)], x_sem.at[1]).wait()
    planes = [spec_buf[i].astype(F32) for i in range(NTM)]
    spec = (planes[0] + planes[1]) + (planes[2] + planes[3])
    high = spec.astype(BF16)
    rest = (spec - high.astype(F32)).astype(BF16)
    lags = dot(jnp.concatenate([high[0:8], rest[0:8]], axis=0), inv_buf[0:1024, :])
    lags = lags + dot(jnp.concatenate([high[8:16], rest[8:16]], axis=0), inv_buf[1024:2048, :])
    out_ref[...] = lags

    landed(send_buf.at[pl.ds(0, NPAIR - 1)], send_sem).wait()
    landed(id_buf.at[pl.ds(0, GROUP - 1)], id_sem.at[0]).wait()
    landed(id_buf.at[pl.ds(0, NPAIR - GROUP)], id_sem.at[2]).wait()
    landed(part_buf.at[pl.ds(0, NPAIR - 1)], part_sem.at[0]).wait()
    landed(spec_buf.at[pl.ds(0, NTM - 1)], x_sem.at[0]).wait()


def on_device(strain, pair_list, pair_bins, bin_slots, seg_valid):
    vmem = pl.BlockSpec(memory_space=pltpu.VMEM)
    smem = pl.BlockSpec(memory_space=pltpu.SMEM)
    hbm = pl.BlockSpec(memory_space=pl.ANY)
    dma = pltpu.SemaphoreType.DMA
    both = pl.pallas_call(
        body,
        out_shape=jax.ShapeDtypeStruct((16, LAGS // NTM), F32),
        in_specs=[hbm, hbm, hbm, hbm, hbm, hbm, smem, smem, smem],
        out_specs=vmem,
        scratch_shapes=[
            pltpu.VMEM((2, 128, SEG_LEN), BF16),
            pltpu.VMEM((512, SUB), BF16),
            pltpu.VMEM((3, 512, 2 * SUB), BF16),
            pltpu.VMEM((2 * BAND, LAGS // NTM), BF16),
            pltpu.VMEM((1024, 128), BF16),
            pltpu.VMEM((2, 4096), jnp.int32),
            pltpu.VMEM((4, 256, 2 * SUB), BF16),
            pltpu.VMEM((4, 512, 256), F32),
            pltpu.VMEM((NPAIR, 64, 128), BF16),
            pltpu.VMEM((NPAIR, 64, 128), BF16),
            pltpu.VMEM((NPAIR, 1, 128), jnp.int32),
            pltpu.VMEM((128, 128), F32),
            pltpu.VMEM((64, 128), F32),
            pltpu.VMEM((64, 128), F32),
            pltpu.VMEM((NPAIR, 128, 256), BF16),
            pltpu.VMEM((NPAIR, 128, 128), BF16),
            pltpu.VMEM((512, 4096), BF16),
            pltpu.VMEM((NPAIR * STEP, 128), F32),
            pltpu.VMEM((4096, 256), BF16),
            pltpu.VMEM((NPAIR, 2, 128), F32),
            pltpu.VMEM((NPAIR, 2, 128), F32),
            pltpu.VMEM((NTM, 16, BAND), BF16),
            dma((11,)), dma, dma((NPAIR,)), dma((4,)), dma((2,)), dma((2,)),
        ],
        compiler_params=pltpu.CompilerParams(
            collective_id=0, has_side_effects=True, vmem_limit_bytes=60 << 20
        ),
    )(
        strain,
        *(jnp.asarray(table) for table in forward_tables()),
        jnp.asarray(inverse_tables()),
        jnp.asarray(fold_table()),
        pair_list.T,
        pair_bins,
        bin_slots,
        seg_valid,
    )
    return both[0:8] + both[8:16]


def solution(mesh):
    return jax.shard_map(
        on_device,
        mesh=mesh,
        in_specs=(P("tm", "pair", None), P(), P("pair"), P(), P("tm")),
        out_specs=P("pair", "tm"),
        check_vma=False,
    )
```

```python
import functools
import math

import jax
import jax.numpy as jnp
import numpy as np
from jax import lax
from jax.experimental import pallas as pl
from jax.experimental.pallas import tpu as pltpu
from jax.sharding import PartitionSpec as P

SEG_LEN = 8192
BAND = 1024
FIRST_BIN = 128
LAGS = 2048
EPS = 1e-06
NPAIR = 64
NTM = 4
STEP = 129
ID_STEP = 16
GROUP = 8
SUB = SEG_LEN // 8
MESH = pl.DeviceIdType.MESH
F32 = jnp.float32
BF16 = jnp.bfloat16


def owned_bins():
    bins = np.zeros((4, 16, 2, 8), np.int64)
    for c in range(4):
        for a in range(2):
            k1 = (0, 4)[a] if c == 0 else (c, 8 - c)[a]
            for w in range(16):
                bins[c, w, a] = k1 + 8 * (16 + 8 * w + np.arange(8))
    return bins


def forward_tables():
    bins = owned_bins()
    t = np.arange(SUB, dtype=np.int64)
    theta = (bins[..., None] * t % SEG_LEN) * (2.0 * math.pi / SEG_LEN)
    cos, sin = np.cos(theta), np.sin(theta)
    table = np.zeros((4, 16, 2, 2, 8, 2, SUB), np.float64)
    sign = (1.0, -1.0)
    for c in range(4):
        for a in range(2):
            if c == 0:
                table[c, :, 0, a, :, a] = cos[c, :, a]
                table[c, :, 1, a, :, a] = -sin[c, :, a]
            else:
                table[c, :, 0, a, :, 0] = cos[c, :, a]
                table[c, :, 0, a, :, 1] = sign[a] * sin[c, :, a]
                table[c, :, 1, a, :, 0] = -sin[c, :, a]
                table[c, :, 1, a, :, 1] = sign[a] * cos[c, :, a]
    first = np.stack([table[0, :, :, a, :, a] for a in range(2)])
    rest = table[1:].reshape(3, 512, 2 * SUB)
    return first.reshape(512, SUB).astype(jnp.bfloat16), rest.astype(jnp.bfloat16)


def inverse_tables():
    bins = owned_bins().reshape(NPAIR, 16)
    lag = np.arange(LAGS, dtype=np.int64) - LAGS // 2
    phi = (bins[..., None] * lag % SEG_LEN) * (2.0 * math.pi / SEG_LEN)
    factor = 1.0 / math.sqrt(BAND)
    table = np.stack([np.cos(phi) * factor, -np.sin(phi) * factor], axis=1)
    table = table.reshape(2 * BAND, NTM, LAGS // NTM).transpose(1, 0, 2)
    return np.ascontiguousarray(table).astype(jnp.bfloat16)


def fold_table():
    table = np.zeros((4, 2, 2, 2, 2, 16, 4, 2, 16), np.float32)
    for q in range(4):
        for b in range(16):
            table[q, 0, 0, :, :, b, q, 0, b] = 1.0
            table[q, 0, 1, :, :, b, q, 0, b] = 1.0
            table[q, 1, 0, :, :, b, q, 1, b] = -1.0
            table[q, 1, 1, :, :, b, q, 1, b] = 1.0
    return table.reshape(1024, 128).astype(jnp.bfloat16)


def iota(shape, dim):
    return lax.broadcasted_iota(jnp.int32, shape, dim)


def dot(a, b):
    return jnp.dot(a, b, preferred_element_type=F32)


def dot_nt(a, b):
    return lax.dot_general(a, b, (((1,), (1,)), ((), ())), preferred_element_type=F32)


def body(
    x_hbm, real_hbm, tab_hbm, inv_hbm, fold_hbm, pairs_hbm, bins_smem, slots_smem, valid_smem,
    out_ref,
    x_buf, real_buf, tab_buf, inv_buf, fold_ref, pairs_ref, y_buf, r_buf, send_buf, recv_buf, id_buf,
    src_rows, loc_rows, loc_mat, g1_buf, g2_buf, s_buf, rows_buf, p_buf,
    part_buf, got_buf, spec_buf,
    load_sem, send_sem, recv_sem, id_sem, part_sem, x_sem,
):
    tm = lax.axis_index("tm")
    me = lax.axis_index("pair")

    def x_load(n):
        rows = pl.ds(n % 2 * 64, 64)
        return pltpu.make_async_copy(x_hbm.at[n // 2, rows], x_buf.at[n // 2, rows], load_sem.at[n])

    def tab_load(c):
        if c == 0:
            return pltpu.make_async_copy(real_hbm, real_buf, load_sem.at[4])
        return pltpu.make_async_copy(tab_hbm.at[c - 1], tab_buf.at[c - 1], load_sem.at[4 + c])

    inv_load = pltpu.make_async_copy(inv_hbm.at[tm], inv_buf, load_sem.at[8])
    fold_load = pltpu.make_async_copy(fold_hbm, fold_ref, load_sem.at[9])
    pairs_load = pltpu.make_async_copy(pairs_hbm, pairs_ref, load_sem.at[10])
    for n in range(4):
        x_load(n).start()
    for c in range(4):
        tab_load(c).start()
    pairs_load.start()
    inv_load.start()
    fold_load.start()

    barrier = pltpu.get_barrier_semaphore()

    def greet(i):
        pl.semaphore_signal(barrier, inc=1, device_id=(tm, lax.rem(me + i, NPAIR)), device_id_type=MESH)

    for i in range(1, 8):
        greet(i)
    for i in range(1, NTM):
        pl.semaphore_signal(barrier, inc=1, device_id=(lax.rem(tm + i, NTM), me), device_id_type=MESH)

    lane = iota((1, 128), 1)
    first_lane = lax.rem(me, 2) * 64

    def one_id(k, row):
        r = slots_smem[bins_smem[k]]
        code = (r & 3) * 128 + (r >> 3) * 2 + ((r >> 2) & 1)
        return jnp.where(lane == first_lane + k, code, row)

    id_buf[me] = lax.fori_loop(0, 64, one_id, jnp.zeros((1, 128), jnp.int32))

    root = math.sqrt(0.5)
    greeted = (8, 24, 40, 52)
    for n in range(4):
        x_load(n).wait()

        def split(step, _, n=n):
            s, some = n // 2, (4, 4, 3, 3)[n]
            for j in range(some):
                greet(greeted[n] + step * some + j)
            rows = pl.ds(pl.multiple_of(n % 2 * 64 + step * 16, 16), 16)
            to = pl.ds(pl.multiple_of(n * 64 + step * 16, 16), 16)
            for h in range(2):
                v = [
                    x_buf[s, rows, e * SUB + h * 512 : e * SUB + h * 512 + 512].astype(F32)
                    for e in range(8)
                ]
                s04, s26, s15, s37 = v[0] + v[4], v[2] + v[6], v[1] + v[5], v[3] + v[7]
                d04, d26, d15, d37 = v[0] - v[4], v[2] - v[6], v[1] - v[5], v[3] - v[7]
                even, odd = s04 + s26, s15 + s37
                diff, both = (d15 - d37) * root, (d15 + d37) * root
                parts = (
                    (even + odd, even - odd),
                    (d04 + diff, -d26 - both),
                    (s04 - s26, s37 - s15),
                    (d04 - diff, d26 - both),
                )
                for c in range(4):
                    for part in range(2):
                        at = part * SUB + h * 512
                        y_buf[c, to, at : at + 512] = parts[c][part].astype(BF16)
            return 0

        lax.fori_loop(0, 4, split, 0)

    here = me // GROUP * GROUP
    mine = lax.rem(me, GROUP)

    def remote(src, dst, sems, to):
        return pltpu.make_async_remote_copy(
            src_ref=src, dst_ref=dst, send_sem=sems[0], recv_sem=sems[1],
            device_id=to, device_id_type=MESH,
        )

    def landed(ref, sem):
        return pltpu.make_async_copy(ref, ref, sem)

    def offset(n):
        return (32 + n // 2 * (1 - n % 2 * 2)) * jnp.minimum(n, 1)

    for c in range(4):
        tab_load(c).wait()
        if c == 0:
            r_buf[0, 0:256] = dot_nt(real_buf[0:256], y_buf[0, :, 0:SUB])
            r_buf[0, 256:512] = dot_nt(real_buf[256:512], y_buf[0, :, SUB : 2 * SUB])
        else:
            r_buf[c] = dot_nt(tab_buf[c - 1], y_buf[c])

    def white(w):
        rows = pl.ds(pl.multiple_of(w * 32, 32), 32)
        both = [r_buf[0, pl.ds(pl.multiple_of(a * 256 + w * 16, 16), 16), :] for a in range(2)]
        real = jnp.concatenate([both[0][0:8], both[1][0:8], both[0][8:16], both[1][8:16]], axis=0)
        parts = [real] + [r_buf[c, rows, :] for c in range(1, 4)]
        power = parts[0] * parts[0]
        for c in range(1, 4):
            power = power + parts[c] * parts[c]
        energy = jnp.sum(power, axis=0, keepdims=True) * (1.0 / 64.0)
        scale = lax.rsqrt(energy + EPS)
        for c in range(4):
            done = (parts[c] * scale).astype(BF16)
            send_buf[c * 16 + w, 0:32, :] = done[:, 0:128]
            send_buf[c * 16 + w, 32:64, :] = done[:, 128:256]

    def white_step(w, _):
        white(w)
        return 0

    lax.fori_loop(0, 16, white_step, 0, unroll=16)

    pl.semaphore_wait(barrier, NPAIR - 1 + NTM - 1)

    for i in range(1, GROUP):
        to = here + lax.rem(mine + i, GROUP)
        remote(id_buf.at[me], id_buf.at[me], (id_sem.at[0], id_sem.at[1]), (tm, to)).start()

    def send_main(n, _):
        d = lax.rem(me + offset(n), NPAIR)
        remote(send_buf.at[d], recv_buf.at[me], (send_sem, recv_sem.at[me]), (tm, d)).start()
        return 0

    lax.fori_loop(1, ID_STEP, send_main, 0)
    landed(id_buf.at[pl.ds(0, GROUP - 1)], id_sem.at[1]).wait()
    own_group = id_buf.at[pl.ds(here, GROUP)]
    for i in range(1, GROUP):
        to = lax.rem(me + i * GROUP, NPAIR)
        remote(own_group, own_group, (id_sem.at[2], id_sem.at[3]), (tm, to)).start()
    lax.fori_loop(ID_STEP, NPAIR, send_main, 0)
    recv_buf[me] = send_buf[me]
    pairs_load.wait()

    low = iota((1, 128), 1) < 64
    for q in range(32):
        a = pairs_ref[0:1, q * 128 : q * 128 + 128]
        b = pairs_ref[1:2, q * 128 : q * 128 + 128]
        first = jnp.where(low, a, pltpu.roll(b, 64, 1))
        second = jnp.where(low, pltpu.roll(a, 64, 1), b)
        for j, row in enumerate((first, second)):
            src_rows[2 * q + j : 2 * q + j + 1, :] = (row >> 6).astype(F32)
            loc_rows[2 * q + j : 2 * q + j + 1, :] = (row & 63).astype(F32)
    src_rows[64:128, :] = jnp.zeros((64, 128), F32)
    src_cols = src_rows[...].T.astype(BF16)
    lane_sq = iota((128, 128), 1)
    sub_sq = iota((128, 128), 0)
    lane_f = lane_sq.astype(F32)
    ones_sq = jnp.ones((128, 128), BF16)
    asks = 8

    def ask(step, _):
        base = step * asks
        pick = (iota((128, asks * 128), 0) == base + iota((128, asks * 128), 1) // 128)
        src_b = dot(src_cols, pick.astype(BF16))
        cols = [src_b[:, j * 128 : j * 128 + 128] for j in range(asks)]
        earlier = []
        for j in range(asks):
            row = src_rows[pl.ds(base + j, 1), :]
            hit = jnp.logical_and(cols[j] == row, lane_sq < sub_sq)
            earlier.append(jnp.where(hit, 1.0, 0.0).astype(BF16))
        slot_b = dot(jnp.concatenate(earlier, axis=0), ones_sq)
        for j in range(asks):
            code = cols[j] + 64.0 * slot_b[j * 128 : j * 128 + 128]
            g2 = jnp.where(code == lane_f, 1.0, 0.0).astype(BF16)
            g2_buf[base + j] = g2
            loc = jnp.broadcast_to(loc_rows[pl.ds(base + j, 1), :], (16, 128)).astype(BF16)
            loc_mat[pl.ds(base + j, 1), :] = dot(loc, g2)[0:1, :]
        return 0

    lax.fori_loop(0, NPAIR // asks, ask, 0)

    loc_cols = loc_mat[...].astype(BF16)

    def choose(s, _):
        pick = iota((128, 256), 0) == s + iota((128, 256), 1) // 128 * 64
        loc_b = dot(loc_cols, pick.astype(BF16))
        loc_b = 2.0 * jnp.concatenate([loc_b[:, 0:128], loc_b[:, 128:256]], axis=0)
        g1_buf[s, :, 0:128] = jnp.where(loc_b == lane_f, 1.0, 0.0).astype(BF16)
        g1_buf[s, :, 128:256] = jnp.where(loc_b + 1.0 == lane_f, 1.0, 0.0).astype(BF16)
        return 0

    lax.fori_loop(0, NPAIR, choose, 0, unroll=8)

    landed(id_buf.at[pl.ds(0, NPAIR - GROUP)], id_sem.at[3]).wait()
    for q in range(32):
        row = id_buf[2 * q] + id_buf[2 * q + 1]
        hit = iota((512, 128), 0) == row
        s_buf[:, q * 128 : q * 128 + 128] = jnp.where(hit, 1.0, 0.0).astype(BF16)

    zero = jnp.zeros((16, 128), BF16)

    batch = 8

    def take(step, _):
        first = step * batch
        sources = [lax.rem(me + NPAIR - offset(first + j), NPAIR) for j in range(batch)]

        @pl.when(first > 0)
        def _():
            landed(recv_buf.at[sources[0]], recv_sem.at[sources[0]]).wait()

        for s in sources[1:]:
            landed(recv_buf.at[s], recv_sem.at[s]).wait()
        for s in sources:
            rows = []
            for ri in range(2):
                for ch in range(2):
                    for g in range(2):
                        at = (2 * g + ri) * 16
                        piece = recv_buf[s, at : at + 16, :]
                        halves = [piece, zero] if ch == 0 else [zero, piece]
                        rows.append(jnp.concatenate(halves, axis=1))
            rows_buf[pl.ds(s * STEP, 128), :] = dot_nt(
                g1_buf[s], jnp.concatenate(rows, axis=0)
            )
        return 0

    lax.fori_loop(0, NPAIR // batch, take, 0)

    def cross(p, _):
        asked = [rows_buf[pl.ds(p + 64 * j, 64, stride=STEP), :] for j in range(2)]
        asked = jnp.concatenate(asked, axis=0).astype(BF16)
        sides = dot(g2_buf[p], asked)
        left, right = sides[0:64], sides[64:128]
        to = pl.ds(pl.multiple_of(p * 64, 64), 64)
        p_buf[to, 0:128] = (left * right).astype(BF16)
        p_buf[to, 128:256] = (left * pltpu.roll(right, 64, 1)).astype(BF16)
        return 0

    lax.fori_loop(0, NPAIR, cross, 0, unroll=16)

    seg = (iota((1, 256), 1) >> 4) & 1
    weight = jnp.where(seg == 0, valid_smem[0], valid_smem[1]).astype(F32)
    fold_load.wait()
    z = dot(s_buf[...], p_buf[...]) * weight
    high = z.astype(BF16)
    rest = (z - high.astype(F32)).astype(BF16)
    total = jnp.zeros((128, 128), F32)
    for q in range(4):
        fold = fold_ref[q * 256 : q * 256 + 256, :]
        part = slice(q * 128, q * 128 + 128)
        total = total + (dot(high[part], fold) + dot(rest[part], fold))
    for d in range(NPAIR):
        part_buf[d] = total[2 * d : 2 * d + 2, :]

    def send_part(n, _):
        d = lax.rem(me + offset(n), NPAIR)
        remote(part_buf.at[d], got_buf.at[me], (part_sem.at[0], part_sem.at[1]), (tm, d)).start()
        return 0

    lax.fori_loop(1, NPAIR, send_part, 0)
    got_buf[me] = part_buf[me]
    landed(got_buf.at[pl.ds(0, NPAIR - 1)], part_sem.at[1]).wait()

    sub8, lane8 = iota((8, 128), 0), iota((8, 128), 1)
    def spread(tile):
        made = jnp.zeros((8, 128), F32)
        for j in range(4):
            d = 4 * tile + j
            two = got_buf[d]
            both = jnp.where(
                sub8 < 4,
                jnp.broadcast_to(two[0:1, :], (8, 128)),
                jnp.broadcast_to(two[1:2, :], (8, 128)),
            )
            for q in range(4):
                turned = pltpu.roll(both, (32 * (j - q)) % 128, 1) if j != q else both
                fits = jnp.logical_and(sub8 % 4 == q, lane8 // 32 == j)
                made = jnp.where(fits, turned, made)
        return made

    for tile in range(8):
        both = jnp.concatenate([spread(tile), spread(tile + 8)], axis=0)
        spec_buf[tm, :, tile * 128 : tile * 128 + 128] = both.astype(BF16)

    own_spec = spec_buf.at[tm]
    for i in range(1, NTM):
        remote(own_spec, own_spec, (x_sem.at[0], x_sem.at[1]), (lax.rem(tm + i, NTM), me)).start()
    inv_load.wait()
    landed(spec_buf.at[pl.ds(0, NTM - 1)], x_sem.at[1]).wait()
    planes = [spec_buf[i].astype(F32) for i in range(NTM)]
    spec = (planes[0] + planes[1]) + (planes[2] + planes[3])
    high = spec.astype(BF16)
    rest = (spec - high.astype(F32)).astype(BF16)
    lags = dot(jnp.concatenate([high[0:8], rest[0:8]], axis=0), inv_buf[0:1024, :])
    lags = lags + dot(jnp.concatenate([high[8:16], rest[8:16]], axis=0), inv_buf[1024:2048, :])
    out_ref[...] = lags

    landed(send_buf.at[pl.ds(0, NPAIR - 1)], send_sem).wait()
    landed(id_buf.at[pl.ds(0, GROUP - 1)], id_sem.at[0]).wait()
    landed(id_buf.at[pl.ds(0, NPAIR - GROUP)], id_sem.at[2]).wait()
    landed(part_buf.at[pl.ds(0, NPAIR - 1)], part_sem.at[0]).wait()
    landed(spec_buf.at[pl.ds(0, NTM - 1)], x_sem.at[0]).wait()


def on_device(strain, pair_list, pair_bins, bin_slots, seg_valid):
    vmem = pl.BlockSpec(memory_space=pltpu.VMEM)
    smem = pl.BlockSpec(memory_space=pltpu.SMEM)
    hbm = pl.BlockSpec(memory_space=pl.ANY)
    dma = pltpu.SemaphoreType.DMA
    both = pl.pallas_call(
        body,
        out_shape=jax.ShapeDtypeStruct((16, LAGS // NTM), F32),
        in_specs=[hbm, hbm, hbm, hbm, hbm, hbm, smem, smem, smem],
        out_specs=vmem,
        scratch_shapes=[
            pltpu.VMEM((2, 128, SEG_LEN), BF16),
            pltpu.VMEM((512, SUB), BF16),
            pltpu.VMEM((3, 512, 2 * SUB), BF16),
            pltpu.VMEM((2 * BAND, LAGS // NTM), BF16),
            pltpu.VMEM((1024, 128), BF16),
            pltpu.VMEM((2, 4096), jnp.int32),
            pltpu.VMEM((4, 256, 2 * SUB), BF16),
            pltpu.VMEM((4, 512, 256), F32),
            pltpu.VMEM((NPAIR, 64, 128), BF16),
            pltpu.VMEM((NPAIR, 64, 128), BF16),
            pltpu.VMEM((NPAIR, 1, 128), jnp.int32),
            pltpu.VMEM((128, 128), F32),
            pltpu.VMEM((64, 128), F32),
            pltpu.VMEM((64, 128), F32),
            pltpu.VMEM((NPAIR, 128, 256), BF16),
            pltpu.VMEM((NPAIR, 128, 128), BF16),
            pltpu.VMEM((512, 4096), BF16),
            pltpu.VMEM((NPAIR * STEP, 128), F32),
            pltpu.VMEM((4096, 256), BF16),
            pltpu.VMEM((NPAIR, 2, 128), F32),
            pltpu.VMEM((NPAIR, 2, 128), F32),
            pltpu.VMEM((NTM, 16, BAND), BF16),
            dma((11,)), dma, dma((NPAIR,)), dma((4,)), dma((2,)), dma((2,)),
        ],
        compiler_params=pltpu.CompilerParams(
            collective_id=0, has_side_effects=True, vmem_limit_bytes=60 << 20
        ),
    )(
        strain,
        *(jnp.asarray(table) for table in forward_tables()),
        jnp.asarray(inverse_tables()),
        jnp.asarray(fold_table()),
        pair_list.T,
        pair_bins,
        bin_slots,
        seg_valid,
    )
    return both[0:8] + both[8:16]


def solution(mesh):
    return jax.shard_map(
        on_device,
        mesh=mesh,
        in_specs=(P("tm", "pair", None), P(), P("pair"), P(), P("tm")),
        out_specs=P("pair", "tm"),
        check_vma=False,
    )
```
